128 devices in a mesh: seq: 64 (over y, z, x_hi, core), head: 2 (over x_lo).
Axes of the slice: x: 4 (x_hi: 2, x_lo: 2; x = x_hi * 2 + x_lo), y: 4, z: 4, core: 2. Of those that a mesh axis runs over, the one named last changes fastest.
Arguments:
- tokens: bfloat16 [16384, 2048], P('seq'), may hold values from -24 to 24
- w_query: bfloat16 [2048, 2048], P(None, 'head'), may hold values from -1 to 1
- w_key: bfloat16 [2048, 2048], P(None, 'head'), may hold values from -1 to 1
- w_value: bfloat16 [2048, 2048], P(None, 'head'), may hold values from -0.125 to 0.125
- w_out: bfloat16 [2048, 2048], P('head'), may hold values from -0.125 to 0.125
- cotangent: bfloat16 [16384, 2048], P('seq', 'head'), may hold values from -6 to 6
Outputs:
- mixed: bfloat16 [16384, 2048], P('seq', 'head')
- input_grad: bfloat16 [16384, 2048], P('seq', 'head')
The draws below stay inside these ranges and needn't reach their ends.
All inputs are finite; a program needn't handle non-finite values.
Results may differ from the reference program's by a relative error of at most 0.013.
The reference program's roundings to bfloat16 on the way (of `attended`, `grad_out` and `grad_logits`) count: a program that leaves them out, or rounds other values in their place, can miss the bound.
Values may be sent and summed in bfloat16 or wider, within the bound.
A program may use at most 128 MiB of HBM per device.

```python
import math
import jax
import jax.numpy as jnp
from jax import lax

D = 2048
HEADS = 16
HEAD_DIM = 128
TOK_DEV = 256
LEVELS = 6
TOKENS = 16384
N_SEQ = 64


def draw_w_query(key, part):
    key = jax.random.fold_in(key, 5)
    own = jnp.clip(jax.random.normal(key, (D, D), jnp.float32), -6.0, 6.0)
    mixed_draw = own
    return (mixed_draw * D ** (-0.5)).astype(jnp.bfloat16)


def draw_w_key(key, part):
    key = jax.random.fold_in(key, 7)
    own = jnp.clip(jax.random.normal(key, (D, D), jnp.float32), -6.0, 6.0)
    mixed_draw = own
    return (mixed_draw * D ** (-0.5)).astype(jnp.bfloat16)


def draw_tokens(key, part):
    key = jax.random.fold_in(key, 11)
    base_key = jax.random.fold_in(key, 0)
    scale_key = jax.random.fold_in(key, 1)
    column_key = jax.random.fold_in(key, 3)
    segment_key = jax.random.fold_in(key, 4)
    segment = min(TOK_DEV, 256)
    base = jnp.clip(jax.random.normal(base_key, (TOKENS, D), jnp.float32), -5.0, 5.0)
    row_scale = jnp.exp(jax.random.uniform(scale_key, (TOKENS, 1), jnp.float32, math.log(0.3), math.log(3.0)))
    column_shift = jnp.clip(jax.random.normal(column_key, (1, D), jnp.float32), -3.0, 3.0)
    segment_shift = jnp.clip(jax.random.normal(segment_key, (TOKENS // segment, 1, D), jnp.float32), -3.0, 3.0)
    varied = (base * row_scale).reshape(TOKENS // segment, segment, D) + segment_shift
    shifted = varied.reshape(TOKENS, D) + column_shift
    return jnp.clip(shifted, -24.0, 24.0).astype(jnp.bfloat16)


def block_scale(own_key, shape, cuts, least, top_value):
    def one(dim, blocks):
        draws = jax.random.uniform(jax.random.fold_in(jax.random.fold_in(own_key, 6), dim), (blocks,), jnp.float32, least / len(cuts), top_value / len(cuts))
        return jnp.repeat(jnp.exp(draws), shape[dim] // blocks).reshape((-1,) + (1,) * (len(shape) - dim - 1))

    level = one(*cuts[0])
    for cut in cuts[1:]:
        level = level * one(*cut)
    return level


def centred(rng, dims, width, most, shards=(), kind=jnp.bfloat16):
    values = width * jax.random.normal(rng, dims, jnp.float32)
    if shards:
        values = values * block_scale(rng, dims, shards, -0.22, 0.18)
    return jnp.clip(values, -most, most).astype(kind)


def setup_inputs(seed: int = 0) -> dict:
    key_of = jax.random.split(jax.random.key(seed), 7)
    return {
        "tokens": draw_tokens(jax.random.fold_in(key_of[6], 71), 0),
        "w_query": draw_w_query(jax.random.fold_in(key_of[6], 71), 0),
        "w_key": draw_w_key(jax.random.fold_in(key_of[6], 71), 0),
        "w_value": centred(key_of[3], (D, D), D ** -0.5, 0.125, ((1, 2),)),
        "w_out": centred(key_of[4], (D, D), D ** -0.5, 0.125, ((0, 2),)),
        "cotangent": centred(key_of[5], (TOKENS, D), 1.0, 6.0, ((0, 64), (1, 2))),
    }


def pool_rows(block):
    widened = block.astype(jnp.float32)
    paired = widened.reshape(widened.shape[:-2] + (widened.shape[-2] // 2, 2, widened.shape[-1]))
    return (0.5 * lax.optimization_barrier(jnp.sum(paired, axis=-2))).astype(jnp.bfloat16)

def spread_rows(grad_in):
    doubled = jnp.broadcast_to(0.5 * grad_in[..., :, None, :], grad_in.shape[:-1] + (2, grad_in.shape[-1]))
    return doubled.reshape(grad_in.shape[:-2] + (2 * grad_in.shape[-2], grad_in.shape[-1]))

def make_bias(tok_rows, half_rows, levels):
    pieces = [jnp.zeros((tok_rows,), jnp.float32)]
    for height in range(levels):
        pieces.append(jnp.full((half_rows,), (height + 1) * math.log(2.0), jnp.float32))
    return jnp.concatenate(pieces)

def split_heads(block, head_count):
    return block.reshape(block.shape[0], head_count, block.shape[1] // head_count).astype(jnp.float32)

def softmax_probs(queries, all_keys, key_bias, head_count):
    logits = jnp.einsum('qhd,khd->hqk', split_heads(queries, head_count), split_heads(all_keys, head_count))
    logits = logits * (1.0 / math.sqrt(HEAD_DIM)) + key_bias
    row_peak = lax.optimization_barrier(jnp.max(logits, axis=-1, keepdims=True))
    exp_terms = jnp.exp(logits - row_peak)
    return exp_terms / lax.optimization_barrier(jnp.sum(exp_terms, axis=-1, keepdims=True))

def attend_forward(probs, all_values, head_count):
    prob_low = probs.astype(jnp.bfloat16).astype(jnp.float32)
    result = jnp.einsum('hqk,khd->qhd', prob_low, split_heads(all_values, head_count))
    return result.reshape(result.shape[0], -1).astype(jnp.bfloat16)

def attend_backward(probs, queries, all_keys, all_values, grad_out, head_count):
    prob_low = probs.astype(jnp.bfloat16).astype(jnp.float32)
    grad_heads = split_heads(grad_out, head_count)
    grad_probs = jnp.einsum('qhd,khd->hqk', grad_heads, split_heads(all_values, head_count))
    grad_values = jnp.einsum('hqk,qhd->khd', prob_low, grad_heads)
    row_dot = lax.optimization_barrier(jnp.sum(probs * grad_probs, axis=-1, keepdims=True))
    grad_logits = (probs * (grad_probs - row_dot) * (1.0 / math.sqrt(HEAD_DIM))).astype(jnp.bfloat16).astype(jnp.float32)
    grad_queries = jnp.einsum('hqk,khd->qhd', grad_logits, split_heads(all_keys, head_count))
    grad_keys = jnp.einsum('hqk,qhd->khd', grad_logits, split_heads(queries, head_count))
    return (grad_queries.reshape(grad_queries.shape[0], -1), grad_keys.reshape(grad_keys.shape[0], -1), grad_values.reshape(grad_values.shape[0], -1))

def reference(tokens, w_query, w_key, w_value, w_out, cotangent):
    head_count = HEADS
    half_rows = TOK_DEV // 2
    queries = jnp.dot(tokens, w_query, preferred_element_type=jnp.float32).astype(jnp.bfloat16)
    key_rows = jnp.dot(tokens, w_key, preferred_element_type=jnp.float32).astype(jnp.bfloat16)
    value_rows = jnp.dot(tokens, w_value, preferred_element_type=jnp.float32).astype(jnp.bfloat16)
    query_blocks = queries.reshape(N_SEQ, TOK_DEV, D)
    key_blocks = key_rows.reshape(N_SEQ, TOK_DEV, D)
    value_blocks = value_rows.reshape(N_SEQ, TOK_DEV, D)
    summary_k = pool_rows(key_blocks)
    summary_v = pool_rows(value_blocks)
    block_index = jnp.arange(N_SEQ, dtype=jnp.int32)
    remote_k = []
    remote_v = []
    for height in range(LEVELS):
        partner = jnp.bitwise_xor(block_index // 2 ** height, 1).astype(jnp.int32)
        remote_k.append(summary_k[partner])
        remote_v.append(summary_v[partner])
        if height + 1 < LEVELS:
            groups = summary_k.shape[0] // 2
            summary_k = pool_rows(summary_k.reshape(groups, 2 * half_rows, D))
            summary_v = pool_rows(summary_v.reshape(groups, 2 * half_rows, D))
    all_keys = jnp.concatenate([key_blocks] + remote_k, axis=1)
    all_values = jnp.concatenate([value_blocks] + remote_v, axis=1)
    key_bias = make_bias(TOK_DEV, half_rows, LEVELS)

    def forward_block(items):
        block_q, block_k, block_v = items
        probs = softmax_probs(block_q, block_k, key_bias, head_count)
        return attend_forward(probs, block_v, head_count)
    attended = lax.map(forward_block, (query_blocks, all_keys, all_values)).reshape(TOKENS, D)
    mixed = jnp.dot(attended, w_out, preferred_element_type=jnp.float32).astype(jnp.bfloat16)
    grad_out = lax.dot_general(cotangent, w_out, (((1,), (1,)), ((), ())), preferred_element_type=jnp.float32).astype(jnp.bfloat16)
    grad_blocks = grad_out.reshape(N_SEQ, TOK_DEV, D)

    def backward_block(items):
        block_q, block_k, block_v, block_g = items
        probs = softmax_probs(block_q, block_k, key_bias, head_count)
        return attend_backward(probs, block_q, block_k, block_v, block_g, head_count)
    grad_q, grad_k, grad_v = lax.map(backward_block, (query_blocks, all_keys, all_values, grad_blocks))
    carried_k = None
    carried_v = None
    for height in reversed(range(LEVELS)):
        first_row = TOK_DEV + height * half_rows
        groups = N_SEQ // 2 ** height
        users_k = grad_k[:, first_row:first_row + half_rows].reshape(groups, 2 ** height, half_rows, D).sum(axis=1)
        users_v = grad_v[:, first_row:first_row + half_rows].reshape(groups, 2 ** height, half_rows, D).sum(axis=1)
        owned_k = users_k.reshape(groups // 2, 2, half_rows, D)[:, ::-1].reshape(groups, half_rows, D)
        owned_v = users_v.reshape(groups // 2, 2, half_rows, D)[:, ::-1].reshape(groups, half_rows, D)
        if height + 1 < LEVELS:
            owned_k = owned_k + spread_rows(carried_k).reshape(groups, half_rows, D)
            owned_v = owned_v + spread_rows(carried_v).reshape(groups, half_rows, D)
        carried_k = owned_k
        carried_v = owned_v
    key_grad = (grad_k[:, :TOK_DEV] + spread_rows(carried_k)).reshape(TOKENS, D).astype(jnp.bfloat16)
    value_grad = (grad_v[:, :TOK_DEV] + spread_rows(carried_v)).reshape(TOKENS, D).astype(jnp.bfloat16)
    query_grad = grad_q.reshape(TOKENS, D).astype(jnp.bfloat16)
    contract = (((1,), (1,)), ((), ()))
    input_grad = lax.dot_general(query_grad, w_query, contract, preferred_element_type=jnp.float32)
    input_grad = input_grad + lax.dot_general(key_grad, w_key, contract, preferred_element_type=jnp.float32)
    input_grad = input_grad + lax.dot_general(value_grad, w_value, contract, preferred_element_type=jnp.float32)
    return (mixed, input_grad.astype(jnp.bfloat16))
```

```python
import math

import jax
import jax.numpy as jnp
from jax import lax
from jax.experimental import pallas as pl
from jax.experimental.pallas import tpu as pltpu
from jax.sharding import PartitionSpec as P

MESH = pl.DeviceIdType.MESH
F32 = jnp.float32
BF16 = jnp.bfloat16
LN2 = math.log(2.0)
SCALE = 1.0 / math.sqrt(128)

TOK = 256
WID = 512
HALF = 1024
L1, L2, L3, YP = 0, 128, 256, 384
ROWS = 640


def level_region(dz, dx):
    return (L2 + dx * 64, 64) if dz == 1 else (L3 + (dz - 2) * 64 + dx * 32, 32)


def plane_region(dz, dx):
    return (YP + (dz * 2 + dx) * 32, 32)


def dot(a, b):
    return jnp.dot(a, b, preferred_element_type=F32)


def dot_t(a, b):
    return lax.dot_general(a, b, (((1,), (1,)), ((), ())), preferred_element_type=F32)


def pool(value):
    n = value.shape[0]
    out = lax.broadcasted_iota(jnp.int32, (n // 2, n), 0)
    inp = lax.broadcasted_iota(jnp.int32, (n // 2, n), 1)
    return dot(jnp.where(inp // 2 == out, 0.5, 0.0).astype(BF16), value).astype(BF16)


def spread(value):
    n = value.shape[0]
    out = lax.broadcasted_iota(jnp.int32, (2 * n, n), 0)
    inp = lax.broadcasted_iota(jnp.int32, (2 * n, n), 1)
    return dot(jnp.where(out // 2 == inp, 0.5, 0.0).astype(BF16), value.astype(BF16))


def t_dot(a, b):
    return lax.dot_general(a, b, (((0,), (0,)), ((), ())), preferred_element_type=F32)


def lanes(i, width):
    return pl.ds(pl.multiple_of(i * width, width), width)


(
    M_TOK0, M_TOK1, M_COTC, M_COTH, M_COTF, M_MIXC, M_MIXH, M_INC, M_INH,
    M_Y, M_X1, M_X2, M_ZO, M_ZW, M_ZX, M_ZY,
    B_X1, B_XA, B_Z, B_ZY, B_Y, N_MSG,
) = (0, 1, 2, 3, 4, 5, 6, 7, 8, 9, 12, 13, 14, 17, 20, 23, 26, 27, 28, 34, 40, 43)


def kernel(
    tok_h, wq_h, wk_h, wv_h, wo_h, cot_h, mix_o, ing_o,
    tok, w, wo, cot, kv, qb, go, p0, p1, p2, p3, p4, wpl, p2x, p3x, ybuf, S,
    pf, E, inv, GP, ypb, att, acc, c_send, c_recv, h_send, h_recv, ic_recv, ih_recv,
    dkv, dp0, dS, sb, RS, xa_s, xa_r, gy_s, gy_r, dq, gk, out_b,
    lsem, ssem, rsem,
):
    s = lax.axis_index("seq")
    hd = lax.axis_index("head")
    c = s % 2

    def flip(bit):
        return (1 - 2 * ((s // bit) % 2)) * bit

    core = (s + flip(1), hd)
    head = (s, 1 - hd)
    xhi = (s + flip(2), hd)
    zdev = {1: (s + flip(4), hd), 2: (s + flip(8), hd), 3: (s + flip(4) + flip(8), hd)}
    ydev = {1: (s + flip(16), hd), 2: (s + flip(32), hd), 3: (s + flip(16) + flip(32), hd)}

    own = pl.ds(pl.multiple_of(hd * HALF, HALF), HALF)
    oth = pl.ds(pl.multiple_of((1 - hd) * HALF, HALF), HALF)
    wcol = pl.ds(pl.multiple_of(c * WID, WID), WID)
    halves = ((own, pl.ds(0, HALF)), (oth, pl.ds(HALF, HALF)))
    lcount = [0]

    def load(src, dst):
        cp = pltpu.make_async_copy(src, dst, lsem.at[lcount[0]])
        lcount[0] += 1
        cp.start()
        return cp

    ld_tok = [load(tok_h.at[:, a], tok.at[pl.ds(0, TOK), b]) for a, b in halves]
    ld_k = [load(wk_h.at[a, wcol], w.at[b, pl.ds(0, WID)]) for a, b in halves]
    ld_v = [load(wv_h.at[a, wcol], w.at[b, pl.ds(WID, WID)]) for a, b in halves]
    ld_q = [load(wq_h.at[a, wcol], w.at[b, pl.ds(2 * WID, WID)]) for a, b in halves]
    ld_cot = load(cot_h, cot.at[pl.ds(0, TOK), pl.ds(0, HALF)])
    ld_o = [load(wo_h.at[wcol, a], wo.at[:, b]) for a, b in halves]

    barrier = pltpu.get_barrier_semaphore()
    partners = [core, head, xhi] + [zdev[k] for k in (1, 2, 3)] + [ydev[k] for k in (1, 2, 3)]
    for d in partners:
        pl.semaphore_signal(barrier, inc=1, device_id=d, device_id_type=MESH)
    pl.semaphore_wait(barrier, len(partners))

    def send(n, src, dst, dev):
        cp = pltpu.make_async_remote_copy(
            src_ref=src, dst_ref=dst, send_sem=ssem.at[n], recv_sem=rsem.at[n],
            device_id=dev, device_id_type=MESH,
        )
        cp.start()
        return cp

    def rows(ref, region):
        return ref.at[pl.ds(*region)]

    s_tok = [
        send(M_TOK0 + i, tok_h.at[:, a], tok.at[pl.ds(TOK, TOK), b], core)
        for i, (a, b) in enumerate(halves)
    ]
    s_cotc = send(M_COTC, cot_h, cot.at[pl.ds(TOK, TOK), pl.ds(0, HALF)], core)
    s_coth = send(M_COTH, cot_h, cot.at[pl.ds(0, TOK), pl.ds(HALF, HALF)], head)

    for cp in ld_tok + ld_k + ld_v:
        cp.wait()

    def kv_tiles(b):
        def body(j, _):
            r = dot(tok[pl.ds(b * TOK, TOK), :], w[:, lanes(j, 256)]).astype(BF16)
            kv[pl.ds(b * TOK, TOK), lanes(j, 256)] = r
            return 0

        lax.fori_loop(0, 4, body, 0)

    kv_tiles(0)
    for cp in s_tok:
        cp.wait_recv()
    kv_tiles(1)

    for b in range(2):
        p0[pl.ds(b * 128, 128), :] = pool(kv[pl.ds(b * TOK, TOK), :])
    p1[...] = pool(p0[...])
    m_x1 = send(M_X1, p1, rows(S, (L1, 128)), xhi)
    p2[...] = pool(p1[...])
    m_zo = [send(M_ZO, p2, rows(S, level_region(1, 0)), zdev[1])]
    p3[...] = pool(p2[...])
    m_zo += [send(M_ZO + k - 1, p3, rows(S, level_region(k, 0)), zdev[k]) for k in (2, 3)]
    p4[...] = pool(p3[...])
    m_y = [send(M_Y + k - 1, p4, ybuf.at[k - 1], ydev[k]) for k in (1, 2, 3)]

    for cp in ld_q:
        cp.wait()

    def q_body(j, _):
        qb[:, lanes(j, 256)] = dot(tok[...], w[:, pl.ds(pl.multiple_of(2 * WID + j * 256, 256), 256)]).astype(BF16)
        return 0

    lax.fori_loop(0, 2, q_body, 0)

    for cp in m_y:
        cp.wait_recv()
    wpl[pl.ds(0, 16), :] = ybuf[0]
    wpl[pl.ds(16, 16), :] = pool(jnp.concatenate([ybuf[1], ybuf[2]], axis=0))
    m_x2 = send(M_X2, wpl, rows(S, plane_region(0, 1)), xhi)
    m_zw = [send(M_ZW + k - 1, wpl, rows(S, plane_region(k, 0)), zdev[k]) for k in (1, 2, 3)]
    S[pl.ds(*plane_region(0, 0)), :] = wpl[...]

    m_x1.wait_recv()
    p2x[...] = pool(S[pl.ds(L1, 128), :])
    m_zx = [send(M_ZX, p2x, rows(S, level_region(1, 1)), zdev[1])]
    p3x[...] = pool(p2x[...])
    m_zx += [send(M_ZX + k - 1, p3x, rows(S, level_region(k, 1)), zdev[k]) for k in (2, 3)]
    m_x2.wait_recv()
    m_zy = [
        send(M_ZY + k - 1, rows(S, plane_region(0, 1)), rows(S, plane_region(k, 1)), zdev[k])
        for k in (1, 2, 3)
    ]

    s_coth.wait_recv()
    s_cotf = send(
        M_COTF, cot.at[pl.ds(0, TOK), pl.ds(HALF, HALF)], cot.at[pl.ds(TOK, TOK), pl.ds(HALF, HALF)], core
    )
    ld_cot.wait()
    for cp in ld_o:
        cp.wait()

    def go_tiles(b):
        def body(j, _):
            go[pl.ds(b * TOK, TOK), lanes(j, 256)] = dot_t(
                cot[pl.ds(b * TOK, TOK), :], wo[lanes(j, 256), :]
            ).astype(BF16)
            return 0

        lax.fori_loop(0, 2, body, 0)

    go_tiles(0)
    s_cotc.wait_recv()
    s_cotf.wait_recv()
    go_tiles(1)

    r_iota = lax.broadcasted_iota(jnp.int32, (256, 256), 0)
    ypb[...] = jnp.where((r_iota // 16) % 2 == 0, 5 * LN2, 6 * LN2).astype(F32)

    for cp in m_zo + m_zw + m_zx + m_zy:
        cp.wait_recv()

    chunks = [
        (0, 256, 0.0), (256, 128, LN2), (384 + L1, 128, 2 * LN2), (384 + L2, 128, 3 * LN2),
        (384 + L3, 128, 4 * LN2), (384 + YP, 256, None),
    ]

    def source(first, size, b, h, value):
        col = pl.ds(pl.multiple_of(h * 128 + value * WID, 128), 128)
        if first == 0:
            return kv[pl.ds(b * TOK, TOK), col]
        if first == 256:
            return p0[pl.ds((1 - b) * 128, 128), col]
        return S[pl.ds(first - 384, size), col]

    def forward(h, _):
        hcol = lanes(h, 128)
        for b in range(2):
            q = qb[pl.ds(b * TOK, TOK), hcol]
            it = h * 2 + b
            peak = None
            for first, size, bias in chunks:
                l = dot_t(source(first, size, b, h, 0), q) * SCALE
                if bias is None:
                    l = l + ypb[...]
                elif bias:
                    l = l + bias
                E[it, pl.ds(first, size), :] = l
                top = jnp.max(l, axis=0, keepdims=True)
                peak = top if peak is None else jnp.maximum(peak, top)
            total = None
            for first, size, bias in chunks:
                e = jnp.exp(E[it, pl.ds(first, size), :] - peak)
                E[it, pl.ds(first, size), :] = e
                part = jnp.sum(e, axis=0, keepdims=True)
                total = part if total is None else total + part
            scale = 1.0 / total
            inv[it] = jnp.broadcast_to(scale, (8, 256))
            a = None
            for first, size, bias in chunks:
                pb = (E[it, pl.ds(first, size), :] * scale).astype(BF16)
                part = t_dot(source(first, size, b, h, 1), pb)
                a = part if a is None else a + part
            att[pl.ds(b * TOK, TOK), hcol] = a.T.astype(BF16)
        return 0

    lax.fori_loop(0, 4, forward, 0)

    def out_tiles(j, _):
        acc[:, lanes(j, 256)] = dot(att[...], wo[:, lanes(j, 256)])
        c_send[:, lanes(j, 256)] = acc[pl.ds(TOK, TOK), lanes(j, 256)].astype(BF16)
        return 0

    lax.fori_loop(0, 8, out_tiles, 0)
    s_mixc = send(M_MIXC, c_send, c_recv, core)

    def backward(h, _):
        hcol = lanes(h, 128)
        vcol = pl.ds(pl.multiple_of(h * 128 + WID, 128), 128)
        for b in range(2):
            q = qb[pl.ds(b * TOK, TOK), hcol]
            g = go[pl.ds(b * TOK, TOK), hcol]
            it = h * 2 + b
            scale = inv[it][0:1, :]
            rd = None
            for first, size, bias in chunks:
                gp = dot_t(source(first, size, b, h, 1), g)
                GP[pl.ds(first, size), :] = gp
                p = E[it, pl.ds(first, size), :] * scale
                E[it, pl.ds(first, size), :] = p
                part = jnp.sum(p * gp, axis=0, keepdims=True)
                rd = part if rd is None else rd + part
            dqt = None
            for first, size, bias in chunks:
                p = E[it, pl.ds(first, size), :]
                dl = (p * (GP[pl.ds(first, size), :] - rd) * SCALE).astype(BF16)
                dvv = dot(p.astype(BF16), g)
                dkk = dot(dl, q)
                part = t_dot(source(first, size, b, h, 0), dl)
                dqt = part if dqt is None else dqt + part
                if first == 0:
                    dkv[pl.ds(b * TOK, TOK), hcol] = dkk
                    dkv[pl.ds(b * TOK, TOK), vcol] = dvv
                elif first == 256:
                    dp0[pl.ds((1 - b) * 128, 128), hcol] = dkk
                    dp0[pl.ds((1 - b) * 128, 128), vcol] = dvv
                elif b == 0:
                    dS[pl.ds(first - 384, size), hcol] = dkk
                    dS[pl.ds(first - 384, size), vcol] = dvv
                else:
                    dkk = dkk + dS[pl.ds(first - 384, size), hcol]
                    dvv = dvv + dS[pl.ds(first - 384, size), vcol]
                    dS[pl.ds(first - 384, size), hcol] = dkk
                    dS[pl.ds(first - 384, size), vcol] = dvv
                    sb[pl.ds(first - 384, size), hcol] = dkk.astype(BF16)
                    sb[pl.ds(first - 384, size), vcol] = dvv.astype(BF16)
            dq[pl.ds(b * TOK, TOK), hcol] = dqt.T.astype(BF16)
        return 0

    lax.fori_loop(0, 4, backward, 0)

    b_z, b_zy = {}, {}
    for dx in (1, 0):
        for k in (1, 2, 3):
            r = level_region(k, dx)
            b_z[k, dx] = send(B_Z + 2 * (k - 1) + dx, rows(sb, r), rows(RS, r), zdev[k])
            r = plane_region(k, dx)
            b_zy[k, dx] = send(B_ZY + 2 * (k - 1) + dx, rows(sb, r), rows(RS, r), zdev[k])
        if dx == 1:
            b_x1 = send(B_X1, rows(sb, (L1, 128)), rows(RS, (L1, 128)), xhi)

    s_mixc.wait_recv()

    def mix_tiles(j, _):
        h_send[:, lanes(j, 256)] = (
            acc[pl.ds(0, TOK), pl.ds(pl.multiple_of(HALF + j * 256, 256), 256)]
            + c_recv[:, pl.ds(pl.multiple_of(HALF + j * 256, 256), 256)].astype(F32)
        ).astype(BF16)
        return 0

    lax.fori_loop(0, 4, mix_tiles, 0)
    s_mixh = send(M_MIXH, h_send, h_recv, head)

    def collect(dx):
        for k in (1, 2, 3):
            b_z[k, dx].wait_recv()
            b_zy[k, dx].wait_recv()
        low = RS[pl.ds(*level_region(2, dx)), :].astype(F32) + RS[pl.ds(*level_region(3, dx)), :].astype(F32)
        top = spread(low) + RS[pl.ds(*level_region(1, dx)), :].astype(F32)
        plane = dS[pl.ds(*plane_region(0, dx)), :]
        for k in (1, 2, 3):
            plane = plane + RS[pl.ds(*plane_region(k, dx)), :].astype(F32)
        return top, plane

    top, plane = collect(1)
    xa_s[pl.ds(0, 64), :] = top.astype(BF16)
    xa_s[pl.ds(64, 32), :] = plane.astype(BF16)
    b_xa = send(B_XA, xa_s, xa_r, xhi)
    top, plane = collect(0)
    pf[pl.ds(0, 64), :] = top
    pf[pl.ds(64, 32), :] = plane

    s_mixh.wait_recv()

    def mix_last(j, _):
        out_b[:, lanes(j, 256)] = (
            acc[pl.ds(0, TOK), lanes(j, 256)]
            + c_recv[:, lanes(j, 256)].astype(F32)
            + h_recv[:, lanes(j, 256)].astype(F32)
        ).astype(BF16)
        return 0

    lax.fori_loop(0, 4, mix_last, 0)
    st_mix = load(out_b, mix_o)

    b_xa.wait_recv()
    top = pf[pl.ds(0, 64), :] + xa_r[pl.ds(0, 64), :].astype(F32)
    plane = pf[pl.ds(64, 32), :] + xa_r[pl.ds(64, 32), :].astype(F32)
    gy_s[0] = plane[0:16].astype(BF16)
    high = spread(plane[16:32])
    gy_s[1] = high[0:16].astype(BF16)
    gy_s[2] = high[16:32].astype(BF16)
    b_y = [send(B_Y + k - 1, gy_s.at[k - 1], gy_r.at[k - 1], ydev[k]) for k in (1, 2, 3)]

    def in_q(j, _):
        acc[:, lanes(j, 256)] = dot_t(dq[...], w[lanes(j, 256), pl.ds(2 * WID, WID)])
        return 0

    lax.fori_loop(0, 8, in_q, 0)

    for cp in b_y:
        cp.wait_recv()
    b_x1.wait_recv()
    g4 = gy_r[0].astype(F32) + gy_r[1].astype(F32) + gy_r[2].astype(F32)
    top = top + spread(spread(g4))
    low = spread(top) + RS[pl.ds(L1, 128), :].astype(F32)
    low = spread(low) + dp0[...]
    for b in range(2):
        gk[pl.ds(b * TOK, TOK), :] = (
            spread(low[b * 128 : (b + 1) * 128]) + dkv[pl.ds(b * TOK, TOK), :]
        ).astype(BF16)

    s_mixc.wait_send()

    def in_tiles(j, _):
        acc[:, lanes(j, 256)] += dot_t(gk[...], w[lanes(j, 256), pl.ds(0, 2 * WID)])
        c_send[:, lanes(j, 256)] = acc[pl.ds(TOK, TOK), lanes(j, 256)].astype(BF16)
        return 0

    lax.fori_loop(0, 8, in_tiles, 0)
    s_inc = send(M_INC, c_send, ic_recv, core)
    s_mixh.wait_send()
    s_inc.wait_recv()

    def inh_tiles(j, _):
        h_send[:, lanes(j, 256)] = (
            acc[pl.ds(0, TOK), pl.ds(pl.multiple_of(HALF + j * 256, 256), 256)]
            + ic_recv[:, pl.ds(pl.multiple_of(HALF + j * 256, 256), 256)].astype(F32)
        ).astype(BF16)
        return 0

    lax.fori_loop(0, 4, inh_tiles, 0)
    s_inh = send(M_INH, h_send, ih_recv, head)
    st_mix.wait()
    s_inh.wait_recv()

    def in_last(j, _):
        out_b[:, lanes(j, 256)] = (
            acc[pl.ds(0, TOK), lanes(j, 256)]
            + ic_recv[:, lanes(j, 256)].astype(F32)
            + ih_recv[:, lanes(j, 256)].astype(F32)
        ).astype(BF16)
        return 0

    lax.fori_loop(0, 4, in_last, 0)
    st_in = load(out_b, ing_o)

    for cp in s_tok + [s_cotc, s_coth, s_cotf, m_x1, m_x2, b_x1, b_xa, s_inc, s_inh]:
        cp.wait_send()
    for cp in m_y + m_zo + m_zw + m_zx + m_zy + b_y + list(b_z.values()) + list(b_zy.values()):
        cp.wait_send()
    st_in.wait()


def per_device(tokens, w_query, w_key, w_value, w_out, cotangent):
    V = pltpu.VMEM
    scratch = [
        V((2 * TOK, 2 * HALF), BF16),
        V((2 * HALF, 3 * WID), BF16),
        V((WID, 2 * HALF), BF16),
        V((2 * TOK, 2 * HALF), BF16),
        V((2 * TOK, 2 * WID), BF16),
        V((2 * TOK, WID), BF16),
        V((2 * TOK, WID), BF16),
        V((256, 2 * WID), BF16),
        V((128, 2 * WID), BF16),
        V((64, 2 * WID), BF16),
        V((32, 2 * WID), BF16),
        V((16, 2 * WID), BF16),
        V((32, 2 * WID), BF16),
        V((64, 2 * WID), BF16),
        V((32, 2 * WID), BF16),
        V((3, 16, 2 * WID), BF16),
        V((ROWS, 2 * WID), BF16),
        V((96, 2 * WID), F32),
        V((8, 1024, 256), F32),
        V((8, 8, 256), F32),
        V((1024, 256), F32),
        V((256, 256), F32),
        V((2 * TOK, WID), BF16),
        V((2 * TOK, 2 * HALF), F32),
        V((TOK, 2 * HALF), BF16),
        V((TOK, 2 * HALF), BF16),
        V((TOK, HALF), BF16),
        V((TOK, HALF), BF16),
        V((TOK, 2 * HALF), BF16),
        V((TOK, HALF), BF16),
        V((2 * TOK, 2 * WID), F32),
        V((256, 2 * WID), F32),
        V((ROWS, 2 * WID), F32),
        V((ROWS, 2 * WID), BF16),
        V((ROWS, 2 * WID), BF16),
        V((96, 2 * WID), BF16),
        V((96, 2 * WID), BF16),
        V((3, 16, 2 * WID), BF16),
        V((3, 16, 2 * WID), BF16),
        V((2 * TOK, WID), BF16),
        V((2 * TOK, 2 * WID), BF16),
        V((TOK, HALF), BF16),
        pltpu.SemaphoreType.DMA((16,)),
        pltpu.SemaphoreType.DMA((N_MSG,)),
        pltpu.SemaphoreType.DMA((N_MSG,)),
    ]
    any_spec = pl.BlockSpec(memory_space=pl.ANY)
    out = jax.ShapeDtypeStruct((TOK, HALF), BF16)
    return pl.pallas_call(
        kernel,
        out_shape=(out, out),
        in_specs=[any_spec] * 6,
        out_specs=(any_spec, any_spec),
        scratch_shapes=scratch,
        compiler_params=pltpu.CompilerParams(
            collective_id=0, has_side_effects=True, vmem_limit_bytes=60 * 2**20
        ),
    )(tokens, w_query, w_key, w_value, w_out, cotangent)


def solution(mesh):
    return jax.shard_map(
        per_device,
        mesh=mesh,
        in_specs=(
            P("seq", None), P(None, "head"), P(None, "head"), P(None, "head"),
            P("head", None), P("seq", "head"),
        ),
        out_specs=(P("seq", "head"), P("seq", "head")),
        check_vma=False,
    )
```

```python
import math

import jax
import jax.numpy as jnp
from jax import lax
from jax.experimental import pallas as pl
from jax.experimental.pallas import tpu as pltpu
from jax.sharding import PartitionSpec as P

MESH = pl.DeviceIdType.MESH
F32 = jnp.float32
BF16 = jnp.bfloat16
LN2 = math.log(2.0)
SCALE = 1.0 / math.sqrt(128)

TOK = 256
WID = 512
HALF = 1024
ROWS = 640


def level_region(dz, dx):
    return (128 + dx * 256, 64) if dz == 1 else (128 + dx * 256 + 32 * dz, 32)


def plane_region(dz, dx):
    return (256 + dx * 256 + 32 * dz, 32)


def dot(a, b):
    return jnp.dot(a, b, preferred_element_type=F32)


def dot_t(a, b):
    return lax.dot_general(a, b, (((1,), (1,)), ((), ())), preferred_element_type=F32)


def pool(value):
    n = value.shape[0]
    out = lax.broadcasted_iota(jnp.int32, (n // 2, n), 0)
    inp = lax.broadcasted_iota(jnp.int32, (n // 2, n), 1)
    return dot(jnp.where(inp // 2 == out, 0.5, 0.0).astype(BF16), value).astype(BF16)


def spread(value):
    n = value.shape[0]
    out = lax.broadcasted_iota(jnp.int32, (2 * n, n), 0)
    inp = lax.broadcasted_iota(jnp.int32, (2 * n, n), 1)
    return dot(jnp.where(out // 2 == inp, 0.5, 0.0).astype(BF16), value.astype(BF16))


def t_dot(a, b):
    return lax.dot_general(a, b, (((0,), (0,)), ((), ())), preferred_element_type=F32)


def lanes(i, width):
    return pl.ds(pl.multiple_of(i * width, width), width)


(
    M_TOK, M_COTC, M_COTH, M_COTF, M_MIXC, M_MIXH, M_INC, M_INH,
    M_Y, M_X1, M_X2, M_ZO, M_ZW, M_ZX, M_ZY,
    B_X1, B_XA, B_Z, B_ZY, B_Y, M_LC, M_LH, N_MSG,
) = (0, 2, 3, 5, 7, 11, 13, 17, 19, 22, 23, 24, 27, 30, 33, 36, 37, 38, 44, 50, 53, 57, 59)


def kernel(
    tok_h, wq_h, wk_h, wv_h, wo_h, cot_h, mix_o, ing_o,
    tok, w, wo, cot, kv, qb, go, p0, p1, p2, p3, p4, wpl, p2x, p3x, ybuf, S,
    pf, E, stat, fin, GP, ypb, att, acc, macc, c_send, c_recv, h_send, h_recv, ic_recv, ih_send, ih_recv,
    lacc, lc_send, lc_recv, lh_send, lh_recv,
    dkv, dp0, dS, sb, RS, xa_s, xa_r, gy_s, gy_r, dq, gk, out_b,
    lsem, ssem, rsem,
):
    s = lax.axis_index("seq")
    hd = lax.axis_index("head")
    c = s % 2

    def flip(bit):
        return (1 - 2 * ((s // bit) % 2)) * bit

    core = (s + flip(1), hd)
    head = (s, 1 - hd)
    xhi = (s + flip(2), hd)
    zdev = {1: (s + flip(4), hd), 2: (s + flip(8), hd), 3: (s + flip(4) + flip(8), hd)}
    ydev = {1: (s + flip(16), hd), 2: (s + flip(32), hd), 3: (s + flip(16) + flip(32), hd)}

    own = pl.ds(pl.multiple_of(hd * HALF, HALF), HALF)
    oth = pl.ds(pl.multiple_of((1 - hd) * HALF, HALF), HALF)
    wcol = pl.ds(pl.multiple_of(c * WID, WID), WID)
    halves = ((own, pl.ds(0, HALF)), (oth, pl.ds(HALF, HALF)))
    lcount = [0]

    def load(src, dst):
        cp = pltpu.make_async_copy(src, dst, lsem.at[lcount[0]])
        lcount[0] += 1
        cp.start()
        return cp

    ld_tok = [load(tok_h.at[:, a], tok.at[pl.ds(0, TOK), b]) for a, b in halves]
    ld_k = [load(wk_h.at[a, wcol], w.at[b, pl.ds(0, WID)]) for a, b in halves]
    ld_v = [load(wv_h.at[a, wcol], w.at[b, pl.ds(WID, WID)]) for a, b in halves]
    ld_q = [load(wq_h.at[a, wcol], w.at[b, pl.ds(2 * WID, WID)]) for a, b in halves]
    ld_cot = load(cot_h, cot.at[pl.ds(0, TOK), pl.ds(0, HALF)])
    ld_o = [load(wo_h.at[wcol, a], wo.at[:, b]) for a, b in halves]

    barrier = pltpu.get_barrier_semaphore()
    partners = [core, head, xhi] + [zdev[k] for k in (1, 2, 3)] + [ydev[k] for k in (1, 2, 3)]
    for d in partners:
        pl.semaphore_signal(barrier, inc=1, device_id=d, device_id_type=MESH)
    pl.semaphore_wait(barrier, len(partners))

    def send(n, src, dst, dev):
        cp = pltpu.make_async_remote_copy(
            src_ref=src, dst_ref=dst, send_sem=ssem.at[n], recv_sem=rsem.at[n],
            device_id=dev, device_id_type=MESH,
        )
        cp.start()
        return cp

    def rows(ref, region):
        return ref.at[pl.ds(*region)]

    s_tok = [
        send(M_TOK + i, tok_h.at[:, a], tok.at[pl.ds(TOK, TOK), b], core)
        for i, (a, b) in enumerate(halves)
    ]
    s_cotc = send(M_COTC, cot_h, cot.at[pl.ds(TOK, TOK), pl.ds(0, HALF)], core)

    COT = [pl.ds(0, 192), pl.ds(192, 64)]

    def send_cot(i):
        part = COT[i]
        return send(M_COTH + i, cot_h.at[part], cot.at[part, pl.ds(HALF, HALF)], head)

    s_coth = [send_cot(0)]

    for cp in ld_tok + ld_k + ld_v:
        cp.wait()

    def kv_tiles(b):
        def body(j, _):
            r = dot(tok[pl.ds(b * TOK, TOK), :], w[:, lanes(j, 256)]).astype(BF16)
            kv[pl.ds(b * TOK, TOK), lanes(j, 256)] = r
            return 0

        lax.fori_loop(0, 4, body, 0)

    kv_tiles(0)
    for cp in s_tok:
        cp.wait_recv()
    kv_tiles(1)

    for b in range(2):
        p0[pl.ds(b * 128, 128), :] = pool(kv[pl.ds(b * TOK, TOK), :])
    p1[...] = pool(p0[...])
    m_x1 = send(M_X1, p1, rows(S, (0, 128)), xhi)
    p2[...] = pool(p1[...])
    m_zo = [send(M_ZO, p2, rows(S, level_region(1, 0)), zdev[1])]
    p3[...] = pool(p2[...])
    m_zo += [send(M_ZO + k - 1, p3, rows(S, level_region(k, 0)), zdev[k]) for k in (2, 3)]
    p4[...] = pool(p3[...])
    m_y = [send(M_Y + k - 1, p4, ybuf.at[k - 1], ydev[k]) for k in (1, 2, 3)]

    for cp in ld_q:
        cp.wait()

    def q_body(j, _):
        qb[:, lanes(j, 256)] = dot(tok[...], w[:, pl.ds(pl.multiple_of(2 * WID + j * 256, 256), 256)]).astype(BF16)
        return 0

    lax.fori_loop(0, 2, q_body, 0)

    groups = [
        [(0, 256, 0.0), (256, 128, LN2)],
        [(384, 128, 2 * LN2)],
        [(512, 256, None)],
        [(768, 256, None)],
    ]
    chunks = [(gr, first, size) for gr in range(4) for first, size, _ in groups[gr]]
    r_iota = lax.broadcasted_iota(jnp.int32, (256, 256), 0)
    r_level = jnp.where(r_iota < 64, 3, jnp.where(r_iota < 128, 4, 5 + (r_iota // 16) % 2))
    ypb[...] = r_level.astype(F32) * LN2

    def source(first, size, b, h, value):
        col = pl.ds(pl.multiple_of(h * 128 + value * WID, 128), 128)
        if first == 0:
            return kv[pl.ds(b * TOK, TOK), col]
        if first == 256:
            return p0[pl.ds((1 - b) * 128, 128), col]
        return S[pl.ds(first - 384, size), col]

    def score(gr, h, b):
        it = h * 2 + b
        q = qb[pl.ds(b * TOK, TOK), lanes(h, 128)]
        parts = []
        peak = None
        for first, size, bias in groups[gr]:
            l = dot_t(source(first, size, b, h, 0), q) * SCALE
            if bias is None:
                l = l + ypb[...]
            elif bias:
                l = l + bias
            parts.append(l)
            top = jnp.max(l, axis=0, keepdims=True)
            peak = top if peak is None else jnp.maximum(peak, top)
        total = None
        for (first, size, _), l in zip(groups[gr], parts):
            e = jnp.exp(l - peak)
            E[it, pl.ds(first, size), :] = e
            part = jnp.sum(e, axis=0, keepdims=True)
            total = part if total is None else total + part
        stat[gr, it, 0:1, :] = peak
        stat[gr, it, 1:2, :] = total

    def grad_score(gr, h, b):
        it = h * 2 + b
        g = go[pl.ds(b * TOK, TOK), lanes(h, 128)]
        total = None
        for first, size, _ in groups[gr]:
            gp = dot_t(source(first, size, b, h, 1), g)
            GP[it, pl.ds(first, size), :] = gp
            part = jnp.sum(E[it, pl.ds(first, size), :] * gp, axis=0, keepdims=True)
            total = part if total is None else total + part
        stat[gr, it, 2:3, :] = total

    def each(*steps):
        def body(h, _):
            for b in range(2):
                for f, gr in steps:
                    f(gr, h, b)
            return 0

        lax.fori_loop(0, 4, body, 0)

    for cp in m_y:
        cp.wait_recv()
    wpl[pl.ds(0, 16), :] = ybuf[0]
    wpl[pl.ds(16, 16), :] = pool(jnp.concatenate([ybuf[1], ybuf[2]], axis=0))
    m_x2 = send(M_X2, wpl, rows(S, plane_region(0, 1)), xhi)
    s_coth.append(send_cot(1))
    m_zw = [send(M_ZW + k - 1, wpl, rows(S, plane_region(k, 0)), zdev[k]) for k in (1, 2, 3)]
    S[pl.ds(*plane_region(0, 0)), :] = wpl[...]

    each((score, 0))

    m_x1.wait_recv()
    p2x[...] = pool(S[pl.ds(0, 128), :])
    m_zx = [send(M_ZX, p2x, rows(S, level_region(1, 1)), zdev[1])]
    p3x[...] = pool(p2x[...])
    m_zx += [send(M_ZX + k - 1, p3x, rows(S, level_region(k, 1)), zdev[k]) for k in (2, 3)]
    each((score, 1))
    m_x2.wait_recv()
    m_zy = [
        send(M_ZY + k - 1, rows(S, plane_region(0, 1)), rows(S, plane_region(k, 1)), zdev[k])
        for k in (1, 2, 3)
    ]

    for cp in m_zo + m_zw:
        cp.wait_recv()
    each((score, 2))

    s_cotf = []
    for i in range(2):
        s_coth[i].wait_recv()
        s_cotf.append(send(
            M_COTF + i, cot.at[COT[i], pl.ds(HALF, HALF)],
            cot.at[pl.ds(TOK + 192 * i, (192, 64)[i]), pl.ds(HALF, HALF)], core,
        ))
    ld_cot.wait()
    for cp in ld_o:
        cp.wait()

    def go_tiles(b):
        def body(j, _):
            go[pl.ds(b * TOK, TOK), lanes(j, 256)] = dot_t(
                cot[pl.ds(b * TOK, TOK), :], wo[lanes(j, 256), :]
            ).astype(BF16)
            return 0

        lax.fori_loop(0, 2, body, 0)

    go_tiles(0)
    s_cotc.wait_recv()
    for cp in s_cotf:
        cp.wait_recv()
    go_tiles(1)

    each((grad_score, 0), (grad_score, 1), (grad_score, 2))

    for cp in m_zx + m_zy:
        cp.wait_recv()

    def finish(h, _):
        for b in range(2):
            it = h * 2 + b
            score(3, h, b)
            grad_score(3, h, b)
            peaks = [stat[gr, it, 0:1, :] for gr in range(4)]
            peak = jnp.maximum(jnp.maximum(peaks[0], peaks[1]), jnp.maximum(peaks[2], peaks[3]))
            scales = [jnp.exp(m - peak) for m in peaks]
            total = sum(f * stat[gr, it, 1:2, :] for gr, f in enumerate(scales))
            scales = [f / total for f in scales]
            for gr, f in enumerate(scales):
                fin[it, gr : gr + 1, :] = f
            fin[it, 4:5, :] = sum(f * stat[gr, it, 2:3, :] for gr, f in enumerate(scales))
            a = None
            for gr, first, size in chunks:
                pb = (E[it, pl.ds(first, size), :] * scales[gr]).astype(BF16)
                part = t_dot(source(first, size, b, h, 1), pb)
                a = part if a is None else a + part
            att[pl.ds(b * TOK, TOK), lanes(h, 128)] = a.T.astype(BF16)
        return 0

    lax.fori_loop(0, 4, finish, 0)

    def cols(i):
        return pl.ds(i * 512, 512)

    def out_piece(i):
        macc[:, cols(i)] = dot(att[pl.ds(0, TOK), :], wo[:, cols(i)])
        c_send[i] = dot(att[pl.ds(TOK, TOK), :], wo[:, cols(i)]).astype(BF16)
        return send(M_MIXC + i, c_send.at[i], c_recv.at[i], core)

    def head_piece(i, cp, total, got, base, src, dst):
        cp.wait_recv()
        src[i] = (total[pl.ds(0, TOK), cols(2 + i)] + got[2 + i].astype(F32)).astype(BF16)
        return send(base + i, src.at[i], dst.at[i], head)

    def last_piece(i, total, got, got_h):
        out_b[:, cols(i)] = (
            total[pl.ds(0, TOK), cols(i)] + got[i].astype(F32) + got_h[i].astype(F32)
        ).astype(BF16)

    s_mixc = {i: out_piece(i) for i in (2, 3, 0, 1)}
    s_mixh = [head_piece(i, s_mixc[2 + i], macc, c_recv, M_MIXH, h_send, h_recv) for i in (0, 1)]

    def backward(h, _):
        hcol = lanes(h, 128)
        vcol = pl.ds(pl.multiple_of(h * 128 + WID, 128), 128)
        for b in range(2):
            q = qb[pl.ds(b * TOK, TOK), hcol]
            g = go[pl.ds(b * TOK, TOK), hcol]
            it = h * 2 + b
            rd = fin[it, 4:5, :]
            dqt = None
            for gr, first, size in chunks:
                p = E[it, pl.ds(first, size), :] * fin[it, gr : gr + 1, :]
                dl = (p * (GP[it, pl.ds(first, size), :] - rd) * SCALE).astype(BF16)
                dvv = dot(p.astype(BF16), g)
                dkk = dot(dl, q)
                part = t_dot(source(first, size, b, h, 0), dl)
                dqt = part if dqt is None else dqt + part
                if first == 0:
                    dkv[pl.ds(b * TOK, TOK), hcol] = dkk
                    dkv[pl.ds(b * TOK, TOK), vcol] = dvv
                elif first == 256:
                    dp0[pl.ds((1 - b) * 128, 128), hcol] = dkk
                    dp0[pl.ds((1 - b) * 128, 128), vcol] = dvv
                elif b == 0:
                    dS[pl.ds(first - 384, size), hcol] = dkk
                    dS[pl.ds(first - 384, size), vcol] = dvv
                else:
                    dkk = dkk + dS[pl.ds(first - 384, size), hcol]
                    dvv = dvv + dS[pl.ds(first - 384, size), vcol]
                    dS[pl.ds(first - 384, size), hcol] = dkk
                    dS[pl.ds(first - 384, size), vcol] = dvv
                    sb[pl.ds(first - 384, size), hcol] = dkk.astype(BF16)
                    sb[pl.ds(first - 384, size), vcol] = dvv.astype(BF16)
            dq[pl.ds(b * TOK, TOK), hcol] = dqt.T.astype(BF16)
        return 0

    lax.fori_loop(0, 4, backward, 0)

    b_z, b_zy = {}, {}
    for dx in (1, 0):
        for k in (1, 2, 3):
            r = level_region(k, dx)
            b_z[k, dx] = send(B_Z + 2 * (k - 1) + dx, rows(sb, r), rows(RS, r), zdev[k])
            r = plane_region(k, dx)
            b_zy[k, dx] = send(B_ZY + 2 * (k - 1) + dx, rows(sb, r), rows(RS, r), zdev[k])

    for b in range(2):
        gk[pl.ds(b * TOK, TOK), :] = (
            spread(dp0[pl.ds(b * 128, 128), :]) + dkv[pl.ds(b * TOK, TOK), :]
        ).astype(BF16)

    def in_early(j, _):
        acc[:, lanes(j, 256)] = dot_t(dq[...], w[lanes(j, 256), pl.ds(2 * WID, WID)]) + dot_t(
            gk[...], w[lanes(j, 256), pl.ds(0, 2 * WID)]
        )
        return 0

    def collect(dx):
        for k in (1, 2, 3):
            b_z[k, dx].wait_recv()
            b_zy[k, dx].wait_recv()
        low = RS[pl.ds(*level_region(2, dx)), :].astype(F32) + RS[pl.ds(*level_region(3, dx)), :].astype(F32)
        top = spread(low) + RS[pl.ds(*level_region(1, dx)), :].astype(F32)
        plane = dS[pl.ds(*plane_region(0, dx)), :]
        for k in (1, 2, 3):
            plane = plane + RS[pl.ds(*plane_region(k, dx)), :].astype(F32)
        return top, plane

    lax.fori_loop(0, 8, in_early, 0)
    for i in range(4):
        s_mixc[i].wait_send()

    def in_piece(i):
        c_send[i] = acc[pl.ds(TOK, TOK), cols(i)].astype(BF16)
        return send(M_INC + i, c_send.at[i], ic_recv.at[i], core)

    s_inc = {i: in_piece(i) for i in (2, 3, 0, 1)}
    top, plane = collect(1)
    xa_s[pl.ds(0, 64), :] = top.astype(BF16)
    xa_s[pl.ds(64, 32), :] = plane.astype(BF16)
    b_xa = send(B_XA, xa_s, xa_r, xhi)
    s_inh = [head_piece(i, s_inc[2 + i], acc, ic_recv, M_INH, ih_send, ih_recv) for i in (0, 1)]
    b_x1 = send(B_X1, rows(sb, (0, 128)), rows(RS, (0, 128)), xhi)
    top, plane = collect(0)
    pf[pl.ds(0, 64), :] = top
    pf[pl.ds(64, 32), :] = plane

    b_xa.wait_recv()
    top = pf[pl.ds(0, 64), :] + xa_r[pl.ds(0, 64), :].astype(F32)
    plane = pf[pl.ds(64, 32), :] + xa_r[pl.ds(64, 32), :].astype(F32)
    gy_s[0] = plane[0:16].astype(BF16)
    high = spread(plane[16:32])
    gy_s[1] = high[0:16].astype(BF16)
    gy_s[2] = high[16:32].astype(BF16)
    b_y = [send(B_Y + k - 1, gy_s.at[k - 1], gy_r.at[k - 1], ydev[k]) for k in (1, 2, 3)]

    for i in (0, 1):
        s_mixc[i].wait_recv()
        s_mixh[i].wait_recv()
        last_piece(i, macc, c_recv, h_recv)
    st_mix = load(out_b, mix_o)

    for cp in b_y:
        cp.wait_recv()
    b_x1.wait_recv()
    g4 = gy_r[0].astype(F32) + gy_r[1].astype(F32) + gy_r[2].astype(F32)
    top = top + spread(spread(g4))
    low = spread(top) + RS[pl.ds(0, 128), :].astype(F32)
    low = low.astype(BF16)
    out_i = lax.broadcasted_iota(jnp.int32, (TOK, 64), 0)
    inp_i = lax.broadcasted_iota(jnp.int32, (TOK, 64), 1)
    quarter = jnp.where(out_i // 4 == inp_i, 0.25, 0.0).astype(BF16)

    def late_piece(i):
        late = dot_t(low, w[cols(i), pl.ds(0, 2 * WID)])
        lacc[:, cols(i)] = late[0:64]
        lc_send[i] = late[64:128].astype(BF16)
        return send(M_LC + i, lc_send.at[i], lc_recv.at[i], core)

    def late_head(i):
        s_lc[2 + i].wait_recv()
        lh_send[i] = (lacc[:, cols(2 + i)] + lc_recv[2 + i].astype(F32)).astype(BF16)
        return send(M_LH + i, lh_send.at[i], lh_recv.at[i], head)

    s_lc = {i: late_piece(i) for i in (2, 3)}
    s_lh = [late_head(0)]
    s_lc[0] = late_piece(0)
    s_lh.append(late_head(1))
    s_lc[1] = late_piece(1)
    st_mix.wait()
    for i in (0, 1):
        s_inc[i].wait_recv()
        s_inh[i].wait_recv()
        s_lc[i].wait_recv()
        s_lh[i].wait_recv()
        late = lacc[:, cols(i)] + lc_recv[i].astype(F32) + lh_recv[i].astype(F32)
        out_b[:, cols(i)] = (
            acc[pl.ds(0, TOK), cols(i)] + ic_recv[i].astype(F32) + ih_recv[i].astype(F32)
            + dot(quarter, late.astype(BF16))
        ).astype(BF16)
    st_in = load(out_b, ing_o)

    for i in (0, 1):
        s_mixh[i].wait_send()
    for cp in s_lh + list(s_lc.values()):
        cp.wait_send()
    for cp in s_tok + s_coth + s_cotf + s_inh + list(s_inc.values()) + [s_cotc, m_x1, m_x2, b_x1, b_xa]:
        cp.wait_send()
    for cp in m_y + m_zo + m_zw + m_zx + m_zy + b_y + list(b_z.values()) + list(b_zy.values()):
        cp.wait_send()
    st_in.wait()


def copy_out(a, b, a_o, b_o):
    a_o[...] = a[...]
    b_o[...] = b[...]


def per_device(tokens, w_query, w_key, w_value, w_out, cotangent):
    V = pltpu.VMEM
    scratch = [
        V((2 * TOK, 2 * HALF), BF16),
        V((2 * HALF, 3 * WID), BF16),
        V((WID, 2 * HALF), BF16),
        V((2 * TOK, 2 * HALF), BF16),
        V((2 * TOK, 2 * WID), BF16),
        V((2 * TOK, WID), BF16),
        V((2 * TOK, WID), BF16),
        V((256, 2 * WID), BF16),
        V((128, 2 * WID), BF16),
        V((64, 2 * WID), BF16),
        V((32, 2 * WID), BF16),
        V((16, 2 * WID), BF16),
        V((32, 2 * WID), BF16),
        V((64, 2 * WID), BF16),
        V((32, 2 * WID), BF16),
        V((3, 16, 2 * WID), BF16),
        V((ROWS, 2 * WID), BF16),
        V((96, 2 * WID), F32),
        V((8, 1024, 256), F32),
        V((4, 8, 8, 256), F32),
        V((8, 8, 256), F32),
        V((8, 1024, 256), F32),
        V((256, 256), F32),
        V((2 * TOK, WID), BF16),
        V((2 * TOK, 2 * HALF), F32),
        V((TOK, 2 * HALF), F32),
        V((4, TOK, 512), BF16),
        V((4, TOK, 512), BF16),
        V((2, TOK, 512), BF16),
        V((2, TOK, 512), BF16),
        V((4, TOK, 512), BF16),
        V((2, TOK, 512), BF16),
        V((2, TOK, 512), BF16),
        V((64, 2 * HALF), F32),
        V((4, 64, 512), BF16),
        V((4, 64, 512), BF16),
        V((2, 64, 512), BF16),
        V((2, 64, 512), BF16),
        V((2 * TOK, 2 * WID), F32),
        V((256, 2 * WID), F32),
        V((ROWS, 2 * WID), F32),
        V((ROWS, 2 * WID), BF16),
        V((ROWS, 2 * WID), BF16),
        V((96, 2 * WID), BF16),
        V((96, 2 * WID), BF16),
        V((3, 16, 2 * WID), BF16),
        V((3, 16, 2 * WID), BF16),
        V((2 * TOK, WID), BF16),
        V((2 * TOK, 2 * WID), BF16),
        V((TOK, HALF), BF16),
        pltpu.SemaphoreType.DMA((16,)),
        pltpu.SemaphoreType.DMA((N_MSG,)),
        pltpu.SemaphoreType.DMA((N_MSG,)),
    ]
    any_spec = pl.BlockSpec(memory_space=pl.ANY)
    out = jax.ShapeDtypeStruct((TOK, HALF), BF16)
    mixed, input_grad = pl.pallas_call(
        kernel,
        out_shape=(out, out),
        in_specs=[any_spec] * 6,
        out_specs=(any_spec, any_spec),
        scratch_shapes=scratch,
        compiler_params=pltpu.CompilerParams(
            collective_id=0, has_side_effects=True, vmem_limit_bytes=60 * 2**20
        ),
    )(tokens, w_query, w_key, w_value, w_out, cotangent)
    return pl.pallas_call(
        copy_out,
        grid=(2,),
        out_shape=(out, out),
        in_specs=[pl.BlockSpec((TOK // 2, HALF), lambda i: (i, 0))] * 2,
        out_specs=[pl.BlockSpec((TOK // 2, HALF), lambda i: (i, 0))] * 2,
    )(mixed, input_grad)


def solution(mesh):
    return jax.shard_map(
        per_device,
        mesh=mesh,
        in_specs=(
            P("seq", None), P(None, "head"), P(None, "head"), P(None, "head"),
            P("head", None), P("seq", "head"),
        ),
        out_specs=(P("seq", "head"), P("seq", "head")),
        check_vma=False,
    )
```

```python
import functools
import math

import jax
import jax.numpy as jnp
from jax import lax
from jax.experimental import pallas as pl
from jax.experimental.pallas import tpu as pltpu
from jax.sharding import PartitionSpec as P

MESH = pl.DeviceIdType.MESH
F32 = jnp.float32
BF16 = jnp.bfloat16
LN2 = math.log(2.0)
SCALE = 1.0 / math.sqrt(128)

TOK = 256
WID = 512
HALF = 1024
ROWS = 640


def level_region(dz, dx):
    return (128 + dx * 256, 64) if dz == 1 else (128 + dx * 256 + 32 * dz, 32)


def plane_region(dz, dx):
    return (256 + dx * 256 + 32 * dz, 32)


def dot(a, b):
    return jnp.dot(a, b, preferred_element_type=F32)


def dot_t(a, b):
    return lax.dot_general(a, b, (((1,), (1,)), ((), ())), preferred_element_type=F32)


def pool(value):
    n = value.shape[0]
    out = lax.broadcasted_iota(jnp.int32, (n // 2, n), 0)
    inp = lax.broadcasted_iota(jnp.int32, (n // 2, n), 1)
    return dot(jnp.where(inp // 2 == out, 0.5, 0.0).astype(BF16), value).astype(BF16)


def spread(value):
    n = value.shape[0]
    out = lax.broadcasted_iota(jnp.int32, (2 * n, n), 0)
    inp = lax.broadcasted_iota(jnp.int32, (2 * n, n), 1)
    return dot(jnp.where(out // 2 == inp, 0.5, 0.0).astype(BF16), value.astype(BF16))


def t_dot(a, b):
    return lax.dot_general(a, b, (((0,), (0,)), ((), ())), preferred_element_type=F32)


def lanes(i, width):
    return pl.ds(pl.multiple_of(i * width, width), width)


(
    M_TOK, M_COTC, M_COTH, M_COTF, M_MIXC, M_MIXH, M_INC, M_INH,
    M_Y, M_X1, M_X2, M_ZO, M_ZW, M_ZX, M_ZY,
    B_XA, B_Z, B_ZY, B_Y, M_LC, M_LH, N_MSG,
) = (0, 2, 3, 5, 7, 11, 13, 17, 19, 22, 23, 24, 27, 30, 33, 36, 37, 49, 61, 64, 68, 70)


def kernel(
    tok_h, wq_h, wk_h, wv_h, wo_h, cot_h, mix_o, ing_o,
    tok, w, wo, cot, kv, qb, go, p0, p1, p2, p3, p4, wpl, p2x, p3x, ybuf, S,
    pf, E, stat, fin, GP, ypb, att, acc, macc, c_send, c_recv, h_send, h_recv, ic_recv, ih_send, ih_recv,
    lacc, lc_send, lc_recv, lh_send, lh_recv,
    dkv, dp0, dS, sb, RS, xa_s, xa_r, gy_s, gy_r, dq, gk, out_b,
    lsem, ssem, rsem,
):
    s = lax.axis_index("seq")
    hd = lax.axis_index("head")
    c = s % 2

    def flip(bit):
        return (1 - 2 * ((s // bit) % 2)) * bit

    core = (s + flip(1), hd)
    head = (s, 1 - hd)
    xhi = (s + flip(2), hd)
    zdev = {1: (s + flip(4), hd), 2: (s + flip(8), hd), 3: (s + flip(4) + flip(8), hd)}
    ydev = {1: (s + flip(16), hd), 2: (s + flip(32), hd), 3: (s + flip(16) + flip(32), hd)}

    own = pl.ds(pl.multiple_of(hd * HALF, HALF), HALF)
    oth = pl.ds(pl.multiple_of((1 - hd) * HALF, HALF), HALF)
    wcol = pl.ds(pl.multiple_of(c * WID, WID), WID)
    halves = ((own, pl.ds(0, HALF)), (oth, pl.ds(HALF, HALF)))
    lcount = [0]

    def load(src, dst):
        cp = pltpu.make_async_copy(src, dst, lsem.at[lcount[0]])
        lcount[0] += 1
        cp.start()
        return cp

    ld_tok = [load(tok_h.at[:, a], tok.at[pl.ds(0, TOK), b]) for a, b in halves]
    ld_k = [load(wk_h.at[a, wcol], w.at[b, pl.ds(0, WID)]) for a, b in halves]
    ld_v = [load(wv_h.at[a, wcol], w.at[b, pl.ds(WID, WID)]) for a, b in halves]
    ld_q = [load(wq_h.at[a, wcol], w.at[b, pl.ds(2 * WID, WID)]) for a, b in halves]
    ld_cot = load(cot_h, cot.at[pl.ds(0, TOK), pl.ds(0, HALF)])
    ld_o = [load(wo_h.at[wcol, a], wo.at[:, b]) for a, b in halves]

    barrier = pltpu.get_barrier_semaphore()
    partners = [core, head, xhi] + [zdev[k] for k in (1, 2, 3)] + [ydev[k] for k in (1, 2, 3)]
    for d in partners:
        pl.semaphore_signal(barrier, inc=1, device_id=d, device_id_type=MESH)
    pl.semaphore_wait(barrier, len(partners))

    def send(n, src, dst, dev):
        cp = pltpu.make_async_remote_copy(
            src_ref=src, dst_ref=dst, send_sem=ssem.at[n], recv_sem=rsem.at[n],
            device_id=dev, device_id_type=MESH,
        )
        cp.start()
        return cp

    def rows(ref, region):
        return ref.at[pl.ds(*region)]

    s_tok = [
        send(M_TOK + i, tok_h.at[:, a], tok.at[pl.ds(TOK, TOK), b], core)
        for i, (a, b) in enumerate(halves)
    ]
    COT = [pl.ds(0, 192), pl.ds(192, 64)]

    def send_cot(i):
        part = COT[i]
        return send(M_COTH + i, cot_h.at[part], cot.at[part, pl.ds(HALF, HALF)], head)

    s_coth = [send_cot(0)]

    for cp in ld_tok + ld_k + ld_v:
        cp.wait()

    def kv_tiles(b):
        def body(j, _):
            r = dot(tok[pl.ds(b * TOK, TOK), :], w[:, lanes(j, 256)]).astype(BF16)
            kv[pl.ds(b * TOK, TOK), lanes(j, 256)] = r
            return 0

        lax.fori_loop(0, 4, body, 0)

    kv_tiles(0)
    for cp in s_tok:
        cp.wait_recv()
    s_cotc = send(M_COTC, cot_h, cot.at[pl.ds(TOK, TOK), pl.ds(0, HALF)], core)
    kv_tiles(1)

    for b in range(2):
        p0[pl.ds(b * 128, 128), :] = pool(kv[pl.ds(b * TOK, TOK), :])
    p1[...] = pool(p0[...])
    m_x1 = send(M_X1, p1, rows(S, (0, 128)), xhi)
    p2[...] = pool(p1[...])
    m_zo = [send(M_ZO, p2, rows(S, level_region(1, 0)), zdev[1])]
    p3[...] = pool(p2[...])
    m_zo += [send(M_ZO + k - 1, p3, rows(S, level_region(k, 0)), zdev[k]) for k in (2, 3)]
    p4[...] = pool(p3[...])
    m_y = [send(M_Y + k - 1, p4, ybuf.at[k - 1], ydev[k]) for k in (1, 2, 3)]

    for cp in ld_q:
        cp.wait()

    def q_body(j, _):
        qb[:, lanes(j, 256)] = dot(tok[...], w[:, pl.ds(pl.multiple_of(2 * WID + j * 256, 256), 256)]).astype(BF16)
        return 0

    lax.fori_loop(0, 2, q_body, 0)

    groups = [
        [(0, 256, 0.0), (256, 128, LN2)],
        [(384, 128, 2 * LN2)],
        [(512, 256, None)],
        [(768, 128, None)],
        [(896, 128, None)],
    ]
    chunks = [(gr, first, size) for gr in range(5) for first, size, _ in groups[gr]]
    r_iota = lax.broadcasted_iota(jnp.int32, (256, 256), 0)
    r_level = jnp.where(r_iota < 64, 3, jnp.where(r_iota < 128, 4, 5 + (r_iota // 16) % 2))
    ypb[...] = r_level.astype(F32) * LN2

    def source(first, size, b, h, value):
        col = pl.ds(pl.multiple_of(h * 128 + value * WID, 128), 128)
        if first == 0:
            return kv[pl.ds(b * TOK, TOK), col]
        if first == 256:
            return p0[pl.ds((1 - b) * 128, 128), col]
        return S[pl.ds(first - 384, size), col]

    def score(gr, h, b):
        it = h * 2 + b
        q = qb[pl.ds(b * TOK, TOK), lanes(h, 128)]
        parts = []
        peak = None
        for first, size, bias in groups[gr]:
            l = dot_t(source(first, size, b, h, 0), q) * SCALE
            if bias is None:
                l = l + ypb[pl.ds((first - 512) % 256, size), :]
            elif bias:
                l = l + bias
            parts.append(l)
            top = jnp.max(l, axis=0, keepdims=True)
            peak = top if peak is None else jnp.maximum(peak, top)
        total = None
        for (first, size, _), l in zip(groups[gr], parts):
            e = jnp.exp(l - peak)
            E[it, pl.ds(first, size), :] = e
            part = jnp.sum(e, axis=0, keepdims=True)
            total = part if total is None else total + part
        stat[gr, it, 0:1, :] = peak
        stat[gr, it, 1:2, :] = total

    def grad_score(gr, h, b):
        it = h * 2 + b
        g = go[pl.ds(b * TOK, TOK), lanes(h, 128)]
        total = None
        for first, size, _ in groups[gr]:
            gp = dot_t(source(first, size, b, h, 1), g)
            GP[it, pl.ds(first, size), :] = gp
            part = jnp.sum(E[it, pl.ds(first, size), :] * gp, axis=0, keepdims=True)
            total = part if total is None else total + part
        stat[gr, it, 2:3, :] = total

    def each(*steps):
        def body(h, _):
            for b in range(2):
                for f, gr in steps:
                    f(gr, h, b)
            return 0

        lax.fori_loop(0, 4, body, 0)

    for cp in m_y:
        cp.wait_recv()
    wpl[pl.ds(0, 16), :] = ybuf[0]
    wpl[pl.ds(16, 16), :] = pool(jnp.concatenate([ybuf[1], ybuf[2]], axis=0))
    m_x2 = send(M_X2, wpl, rows(S, plane_region(0, 1)), xhi)
    m_zw = [send(M_ZW + k - 1, wpl, rows(S, plane_region(k, 0)), zdev[k]) for k in (1, 2, 3)]
    S[pl.ds(*plane_region(0, 0)), :] = wpl[...]

    each((score, 0))

    m_x1.wait_recv()
    p2x[...] = pool(S[pl.ds(0, 128), :])
    m_zx = [send(M_ZX, p2x, rows(S, level_region(1, 1)), zdev[1])]
    p3x[...] = pool(p2x[...])
    m_zx += [send(M_ZX + k - 1, p3x, rows(S, level_region(k, 1)), zdev[k]) for k in (2, 3)]
    each((score, 1))
    m_x2.wait_recv()
    s_coth.append(send_cot(1))
    m_zy = [
        send(M_ZY + k - 1, rows(S, plane_region(0, 1)), rows(S, plane_region(k, 1)), zdev[k])
        for k in (1, 2, 3)
    ]

    for cp in m_zo + m_zw:
        cp.wait_recv()
    each((score, 2))

    s_cotf = []
    for i in range(2):
        s_coth[i].wait_recv()
        s_cotf.append(send(
            M_COTF + i, cot.at[COT[i], pl.ds(HALF, HALF)],
            cot.at[pl.ds(TOK + 192 * i, (192, 64)[i]), pl.ds(HALF, HALF)], core,
        ))
    ld_cot.wait()
    for cp in ld_o:
        cp.wait()

    def go_tiles(b):
        def body(j, _):
            go[pl.ds(b * TOK, TOK), lanes(j, 256)] = dot_t(
                cot[pl.ds(b * TOK, TOK), :], wo[lanes(j, 256), :]
            ).astype(BF16)
            return 0

        lax.fori_loop(0, 2, body, 0)

    go_tiles(0)
    s_cotc.wait_recv()
    for cp in s_cotf:
        cp.wait_recv()
    go_tiles(1)

    each((grad_score, 0), (grad_score, 1), (grad_score, 2))

    for cp in m_zx:
        cp.wait_recv()
    each((score, 3), (grad_score, 3))
    for cp in m_zy:
        cp.wait_recv()

    def finish(h, _):
        for b in range(2):
            it = h * 2 + b
            score(4, h, b)
            grad_score(4, h, b)
            peaks = [stat[gr, it, 0:1, :] for gr in range(5)]
            peak = functools.reduce(jnp.maximum, peaks)
            scales = [jnp.exp(m - peak) for m in peaks]
            total = sum(f * stat[gr, it, 1:2, :] for gr, f in enumerate(scales))
            scales = [f / total for f in scales]
            for gr, f in enumerate(scales):
                fin[it, gr : gr + 1, :] = f
            fin[it, 5:6, :] = sum(f * stat[gr, it, 2:3, :] for gr, f in enumerate(scales))
            a = None
            for gr, first, size in chunks:
                pb = (E[it, pl.ds(first, size), :] * scales[gr]).astype(BF16)
                part = t_dot(source(first, size, b, h, 1), pb)
                a = part if a is None else a + part
            att[pl.ds(b * TOK, TOK), lanes(h, 128)] = a.T.astype(BF16)
        return 0

    lax.fori_loop(0, 4, finish, 0)

    def cols(i):
        return pl.ds(i * 512, 512)

    def out_piece(i):
        macc[:, cols(i)] = dot(att[pl.ds(0, TOK), :], wo[:, cols(i)])
        c_send[i] = dot(att[pl.ds(TOK, TOK), :], wo[:, cols(i)]).astype(BF16)
        return send(M_MIXC + i, c_send.at[i], c_recv.at[i], core)

    def head_piece(i, cp, total, got, base, src, dst):
        cp.wait_recv()
        src[i] = (total[pl.ds(0, TOK), cols(2 + i)] + got[2 + i].astype(F32)).astype(BF16)
        return send(base + i, src.at[i], dst.at[i], head)

    def last_piece(i, total, got, got_h):
        out_b[:, cols(i)] = (
            total[pl.ds(0, TOK), cols(i)] + got[i].astype(F32) + got_h[i].astype(F32)
        ).astype(BF16)

    s_mixc = {i: out_piece(i) for i in (2, 3, 0, 1)}
    s_mixh = [head_piece(i, s_mixc[2 + i], macc, c_recv, M_MIXH, h_send, h_recv) for i in (0, 1)]

    def backward(pair, i):
        h = 2 * pair + i
        hcol = lanes(h, 128)
        vcol = pl.ds(pl.multiple_of(h * 128 + WID, 128), 128)
        for b in range(2):
            q = qb[pl.ds(b * TOK, TOK), hcol]
            g = go[pl.ds(b * TOK, TOK), hcol]
            it = h * 2 + b
            rd = fin[it, 5:6, :]
            dqt = None
            for gr, first, size in chunks:
                p = E[it, pl.ds(first, size), :] * fin[it, gr : gr + 1, :]
                dl = (p * (GP[it, pl.ds(first, size), :] - rd) * SCALE).astype(BF16)
                dvv = dot(p.astype(BF16), g)
                dkk = dot(dl, q)
                part = t_dot(source(first, size, b, h, 0), dl)
                dqt = part if dqt is None else dqt + part
                if first == 0:
                    dkv[pl.ds(b * TOK, TOK), hcol] = dkk
                    dkv[pl.ds(b * TOK, TOK), vcol] = dvv
                elif first == 256:
                    dp0[pl.ds((1 - b) * 128, 128), hcol] = dkk
                    dp0[pl.ds((1 - b) * 128, 128), vcol] = dvv
                elif b == 0:
                    dS[pl.ds(first - 384, size), hcol] = dkk
                    dS[pl.ds(first - 384, size), vcol] = dvv
                else:
                    dkk = dkk + dS[pl.ds(first - 384, size), hcol]
                    dvv = dvv + dS[pl.ds(first - 384, size), vcol]
                    dS[pl.ds(first - 384, size), hcol] = dkk
                    dS[pl.ds(first - 384, size), vcol] = dvv
                    if first > 384:
                        sb[pair, pl.ds(first - 384, size), lanes(i, 128)] = dkk.astype(BF16)
                        sb[pair, pl.ds(first - 384, size), lanes(i + 2, 128)] = dvv.astype(BF16)
            dq[pl.ds(b * TOK, TOK), hcol] = dqt.T.astype(BF16)

    def heads(pair):
        def body(i, _):
            backward(pair, i)
            return 0

        lax.fori_loop(0, 2, body, 0)

    b_z = {0: [], 1: []}

    def send_z(pair, dx):
        for k in (1, 2, 3):
            for base, r in ((B_Z, level_region(k, dx)), (B_ZY, plane_region(k, dx))):
                n = base + 4 * (k - 1) + 2 * dx + pair
                b_z[dx].append(send(n, rows(sb.at[pair], r), rows(RS.at[pair], r), zdev[k]))

    heads(0)
    send_z(0, 1)
    heads(1)
    send_z(1, 1)
    send_z(0, 0)
    send_z(1, 0)

    for b in range(2):
        gk[pl.ds(b * TOK, TOK), :] = (
            spread(dp0[pl.ds(b * 128, 128), :]) + dkv[pl.ds(b * TOK, TOK), :]
        ).astype(BF16)

    def in_early(j, _):
        acc[:, lanes(j, 256)] = dot_t(dq[...], w[lanes(j, 256), pl.ds(2 * WID, WID)]) + dot_t(
            gk[...], w[lanes(j, 256), pl.ds(0, 2 * WID)]
        )
        return 0

    def returned(region):
        a, b = RS[0, pl.ds(*region), :], RS[1, pl.ds(*region), :]
        return jnp.concatenate([a[:, :256], b[:, :256], a[:, 256:], b[:, 256:]], axis=1).astype(F32)

    def collect(dx):
        for cp in b_z[dx]:
            cp.wait_recv()
        low = returned(level_region(2, dx)) + returned(level_region(3, dx))
        top = spread(low) + returned(level_region(1, dx))
        plane = dS[pl.ds(*plane_region(0, dx)), :]
        for k in (1, 2, 3):
            plane = plane + returned(plane_region(k, dx))
        return top, plane

    lax.fori_loop(0, 8, in_early, 0)
    for i in range(4):
        s_mixc[i].wait_send()

    def in_piece(i):
        c_send[i] = acc[pl.ds(TOK, TOK), cols(i)].astype(BF16)
        return send(M_INC + i, c_send.at[i], ic_recv.at[i], core)

    s_inc = {i: in_piece(i) for i in (2, 3, 0, 1)}
    top, plane = collect(1)
    xa_s[pl.ds(0, 128), :] = (spread(top) + dS[pl.ds(0, 128), :]).astype(BF16)
    xa_s[pl.ds(128, 32), :] = plane.astype(BF16)
    b_xa = send(B_XA, xa_s, xa_r, xhi)
    s_inh = [head_piece(i, s_inc[2 + i], acc, ic_recv, M_INH, ih_send, ih_recv) for i in (0, 1)]
    top, plane = collect(0)
    pf[pl.ds(0, 64), :] = top
    pf[pl.ds(64, 32), :] = plane

    b_xa.wait_recv()
    top = pf[pl.ds(0, 64), :]
    plane = pf[pl.ds(64, 32), :] + xa_r[pl.ds(128, 32), :].astype(F32)
    gy_s[0] = plane[0:16].astype(BF16)
    high = spread(plane[16:32])
    gy_s[1] = high[0:16].astype(BF16)
    gy_s[2] = high[16:32].astype(BF16)
    b_y = [send(B_Y + k - 1, gy_s.at[k - 1], gy_r.at[k - 1], ydev[k]) for k in (1, 2, 3)]

    for i in (0, 1):
        s_mixc[i].wait_recv()
        s_mixh[i].wait_recv()
        last_piece(i, macc, c_recv, h_recv)
    st_mix = load(out_b, mix_o)

    for cp in b_y:
        cp.wait_recv()
    g4 = gy_r[0].astype(F32) + gy_r[1].astype(F32) + gy_r[2].astype(F32)
    top = top + spread(spread(g4))
    low = spread(top) + xa_r[pl.ds(0, 128), :].astype(F32)
    low = low.astype(BF16)
    out_i = lax.broadcasted_iota(jnp.int32, (TOK, 64), 0)
    inp_i = lax.broadcasted_iota(jnp.int32, (TOK, 64), 1)
    quarter = jnp.where(out_i // 4 == inp_i, 0.25, 0.0).astype(BF16)

    def late_piece(i):
        late = dot_t(low, w[cols(i), pl.ds(0, 2 * WID)])
        lacc[:, cols(i)] = late[0:64]
        lc_send[i] = late[64:128].astype(BF16)
        return send(M_LC + i, lc_send.at[i], lc_recv.at[i], core)

    def late_head(i):
        s_lc[2 + i].wait_recv()
        lh_send[i] = (lacc[:, cols(2 + i)] + lc_recv[2 + i].astype(F32)).astype(BF16)
        return send(M_LH + i, lh_send.at[i], lh_recv.at[i], head)

    s_lc = {i: late_piece(i) for i in (2, 3)}
    s_lh = [late_head(0)]
    s_lc[0] = late_piece(0)
    s_lh.append(late_head(1))
    s_lc[1] = late_piece(1)
    st_mix.wait()
    for i in (0, 1):
        s_inc[i].wait_recv()
        s_inh[i].wait_recv()
        s_lc[i].wait_recv()
        s_lh[i].wait_recv()
        late = lacc[:, cols(i)] + lc_recv[i].astype(F32) + lh_recv[i].astype(F32)
        out_b[:, cols(i)] = (
            acc[pl.ds(0, TOK), cols(i)] + ic_recv[i].astype(F32) + ih_recv[i].astype(F32)
            + dot(quarter, late.astype(BF16))
        ).astype(BF16)
    st_in = load(out_b, ing_o)

    for i in (0, 1):
        s_mixh[i].wait_send()
    for cp in s_lh + list(s_lc.values()):
        cp.wait_send()
    for cp in s_tok + s_coth + s_cotf + s_inh + list(s_inc.values()) + [s_cotc, m_x1, m_x2, b_xa]:
        cp.wait_send()
    for cp in m_y + m_zo + m_zw + m_zx + m_zy + b_y + b_z[0] + b_z[1]:
        cp.wait_send()
    st_in.wait()


def copy_out(a, b, a_o, b_o):
    a_o[...] = a[...]
    b_o[...] = b[...]


def per_device(tokens, w_query, w_key, w_value, w_out, cotangent):
    V = pltpu.VMEM
    scratch = [
        V((2 * TOK, 2 * HALF), BF16),
        V((2 * HALF, 3 * WID), BF16),
        V((WID, 2 * HALF), BF16),
        V((2 * TOK, 2 * HALF), BF16),
        V((2 * TOK, 2 * WID), BF16),
        V((2 * TOK, WID), BF16),
        V((2 * TOK, WID), BF16),
        V((256, 2 * WID), BF16),
        V((128, 2 * WID), BF16),
        V((64, 2 * WID), BF16),
        V((32, 2 * WID), BF16),
        V((16, 2 * WID), BF16),
        V((32, 2 * WID), BF16),
        V((64, 2 * WID), BF16),
        V((32, 2 * WID), BF16),
        V((3, 16, 2 * WID), BF16),
        V((ROWS, 2 * WID), BF16),
        V((96, 2 * WID), F32),
        V((8, 1024, 256), F32),
        V((5, 8, 8, 256), F32),
        V((8, 8, 256), F32),
        V((8, 1024, 256), F32),
        V((256, 256), F32),
        V((2 * TOK, WID), BF16),
        V((2 * TOK, 2 * HALF), F32),
        V((TOK, 2 * HALF), F32),
        V((4, TOK, 512), BF16),
        V((4, TOK, 512), BF16),
        V((2, TOK, 512), BF16),
        V((2, TOK, 512), BF16),
        V((4, TOK, 512), BF16),
        V((2, TOK, 512), BF16),
        V((2, TOK, 512), BF16),
        V((64, 2 * HALF), F32),
        V((4, 64, 512), BF16),
        V((4, 64, 512), BF16),
        V((2, 64, 512), BF16),
        V((2, 64, 512), BF16),
        V((2 * TOK, 2 * WID), F32),
        V((256, 2 * WID), F32),
        V((ROWS, 2 * WID), F32),
        V((2, ROWS, WID), BF16),
        V((2, ROWS, WID), BF16),
        V((160, 2 * WID), BF16),
        V((160, 2 * WID), BF16),
        V((3, 16, 2 * WID), BF16),
        V((3, 16, 2 * WID), BF16),
        V((2 * TOK, WID), BF16),
        V((2 * TOK, 2 * WID), BF16),
        V((TOK, HALF), BF16),
        pltpu.SemaphoreType.DMA((16,)),
        pltpu.SemaphoreType.DMA((N_MSG,)),
        pltpu.SemaphoreType.DMA((N_MSG,)),
    ]
    any_spec = pl.BlockSpec(memory_space=pl.ANY)
    out = jax.ShapeDtypeStruct((TOK, HALF), BF16)
    mixed, input_grad = pl.pallas_call(
        kernel,
        out_shape=(out, out),
        in_specs=[any_spec] * 6,
        out_specs=(any_spec, any_spec),
        scratch_shapes=scratch,
        compiler_params=pltpu.CompilerParams(
            collective_id=0, has_side_effects=True, vmem_limit_bytes=60 * 2**20
        ),
    )(tokens, w_query, w_key, w_value, w_out, cotangent)
    return pl.pallas_call(
        copy_out,
        grid=(2,),
        out_shape=(out, out),
        in_specs=[pl.BlockSpec((TOK // 2, HALF), lambda i: (i, 0))] * 2,
        out_specs=[pl.BlockSpec((TOK // 2, HALF), lambda i: (i, 0))] * 2,
    )(mixed, input_grad)


def solution(mesh):
    return jax.shard_map(
        per_device,
        mesh=mesh,
        in_specs=(
            P("seq", None), P(None, "head"), P(None, "head"), P(None, "head"),
            P("head", None), P("seq", "head"),
        ),
        out_specs=(P("seq", "head"), P("seq", "head")),
        check_vma=False,
    )
```

```python
import functools
import math

import jax
import jax.numpy as jnp
from jax import lax
from jax.experimental import pallas as pl
from jax.experimental.pallas import tpu as pltpu
from jax.sharding import PartitionSpec as P

MESH = pl.DeviceIdType.MESH
F32 = jnp.float32
BF16 = jnp.bfloat16
LN2 = math.log(2.0)
SCALE = 1.0 / math.sqrt(128)

TOK = 256
WID = 512
HALF = 1024
ROWS = 640


def level_region(dz, dx):
    return (128 + dx * 256, 64) if dz == 1 else (128 + dx * 256 + 32 * dz, 32)


def half(region, b):
    return (region[0] + b * region[1] // 2, region[1] // 2)


def plane_region(dz, dx):
    return (256 + dx * 256 + 32 * dz, 32)


def dot(a, b):
    return jnp.dot(a, b, preferred_element_type=F32)


def dot_t(a, b):
    return lax.dot_general(a, b, (((1,), (1,)), ((), ())), preferred_element_type=F32)


def pool(value):
    n = value.shape[0]
    out = lax.broadcasted_iota(jnp.int32, (n // 2, n), 0)
    inp = lax.broadcasted_iota(jnp.int32, (n // 2, n), 1)
    return dot(jnp.where(inp // 2 == out, 0.5, 0.0).astype(BF16), value).astype(BF16)


def spread(value):
    n = value.shape[0]
    out = lax.broadcasted_iota(jnp.int32, (2 * n, n), 0)
    inp = lax.broadcasted_iota(jnp.int32, (2 * n, n), 1)
    return dot(jnp.where(out // 2 == inp, 0.5, 0.0).astype(BF16), value.astype(BF16))


def t_dot(a, b):
    return lax.dot_general(a, b, (((0,), (0,)), ((), ())), preferred_element_type=F32)


def lanes(i, width):
    return pl.ds(pl.multiple_of(i * width, width), width)


(
    M_TOK, M_COTC, M_COTH, M_COTF, M_MIXC, M_MIXH, M_INC, M_INH,
    M_Y, M_X1, M_X2, M_ZO, M_ZW, M_ZX, M_ZY,
    B_XA, B_Z, B_ZY, B_Y, M_LC, M_LH, N_MSG,
) = (0, 2, 3, 5, 7, 11, 13, 17, 19, 22, 24, 25, 31, 34, 40, 43, 44, 56, 68, 71, 75, 77)


def kernel(
    tok_h, wq_h, wk_h, wv_h, wo_h, cot_h, mix_o, ing_o,
    tok, w, wo, cot, kv, qb, go, p0, p1, p2, p3, p4, wpl, p2x, p3x, ybuf, S,
    pf, E, stat, fin, GP, ypb, att, acc, macc, c_send, c_recv, h_send, h_recv, ic_recv, ih_send, ih_recv,
    lacc, lc_send, lc_recv, lh_send, lh_recv,
    dkv, dp0, dS, sb, RS, xa_s, xa_r, gy_s, gy_r, dq, gk, out_b,
    lsem, ssem, rsem,
):
    s = lax.axis_index("seq")
    hd = lax.axis_index("head")
    c = s % 2

    def flip(bit):
        return (1 - 2 * ((s // bit) % 2)) * bit

    core = (s + flip(1), hd)
    head = (s, 1 - hd)
    xhi = (s + flip(2), hd)
    zdev = {1: (s + flip(4), hd), 2: (s + flip(8), hd), 3: (s + flip(4) + flip(8), hd)}
    ydev = {1: (s + flip(16), hd), 2: (s + flip(32), hd), 3: (s + flip(16) + flip(32), hd)}

    own = pl.ds(pl.multiple_of(hd * HALF, HALF), HALF)
    oth = pl.ds(pl.multiple_of((1 - hd) * HALF, HALF), HALF)
    wcol = pl.ds(pl.multiple_of(c * WID, WID), WID)
    halves = ((own, pl.ds(0, HALF)), (oth, pl.ds(HALF, HALF)))
    lcount = [0]

    def load(src, dst):
        cp = pltpu.make_async_copy(src, dst, lsem.at[lcount[0]])
        lcount[0] += 1
        cp.start()
        return cp

    ld_tok = [load(tok_h.at[:, a], tok.at[pl.ds(0, TOK), b]) for a, b in halves]
    ld_k = [load(wk_h.at[a, wcol], w.at[b, pl.ds(0, WID)]) for a, b in halves]
    ld_v = [load(wv_h.at[a, wcol], w.at[b, pl.ds(WID, WID)]) for a, b in halves]

    barrier = pltpu.get_barrier_semaphore()
    partners = [core, head, xhi] + [zdev[k] for k in (1, 2, 3)] + [ydev[k] for k in (1, 2, 3)]
    for d in partners:
        pl.semaphore_signal(barrier, inc=1, device_id=d, device_id_type=MESH)
    pl.semaphore_wait(barrier, len(partners))

    def send(n, src, dst, dev):
        cp = pltpu.make_async_remote_copy(
            src_ref=src, dst_ref=dst, send_sem=ssem.at[n], recv_sem=rsem.at[n],
            device_id=dev, device_id_type=MESH,
        )
        cp.start()
        return cp

    def rows(ref, region):
        return ref.at[pl.ds(*region)]

    s_tok = [
        send(M_TOK + i, tok_h.at[:, a], tok.at[pl.ds(TOK, TOK), b], core)
        for i, (a, b) in enumerate(halves)
    ]
    COT = [pl.ds(0, 96), pl.ds(96, 160)]

    def send_cot(i):
        part = COT[i]
        return send(M_COTH + i, cot_h.at[part], cot.at[part, pl.ds(HALF, HALF)], head)

    s_coth = [send_cot(0)]

    for cp in ld_tok + ld_k + ld_v:
        cp.wait()
    ld_q = [load(wq_h.at[a, wcol], w.at[b, pl.ds(2 * WID, WID)]) for a, b in halves]
    ld_cot = load(cot_h, cot.at[pl.ds(0, TOK), pl.ds(0, HALF)])
    ld_o = [load(wo_h.at[wcol, a], wo.at[:, b]) for a, b in halves]

    def kv_tiles(b):
        def body(j, _):
            r = dot(tok[pl.ds(b * TOK, TOK), :], w[:, lanes(j, 256)]).astype(BF16)
            kv[pl.ds(b * TOK, TOK), lanes(j, 256)] = r
            return 0

        lax.fori_loop(0, 4, body, 0)

    m_x1, m_zo, m_zx = [], [], []

    def pool_block(b):
        p0[pl.ds(b * 128, 128), :] = pool(kv[pl.ds(b * TOK, TOK), :])
        p1[pl.ds(b * 64, 64), :] = pool(p0[pl.ds(b * 128, 128), :])
        m_x1.append(send(M_X1 + b, rows(p1, (b * 64, 64)), rows(S, (b * 64, 64)), xhi))
        p2[pl.ds(b * 32, 32), :] = pool(p1[pl.ds(b * 64, 64), :])
        p3[pl.ds(b * 16, 16), :] = pool(p2[pl.ds(b * 32, 32), :])
        m_zo.extend(pass_z(M_ZO, b, 0, p2, p3))

    def pass_z(base, b, dx, two, three):
        out = []
        for k in (1, 2, 3):
            src = rows(two, (b * 32, 32)) if k == 1 else rows(three, (b * 16, 16))
            out.append(send(base + 2 * (k - 1) + b, src, rows(S, half(level_region(k, dx), b)), zdev[k]))
        return out

    kv_tiles(0)
    pool_block(0)
    for cp in s_tok:
        cp.wait_recv()
    s_cotc = send(M_COTC, cot_h, cot.at[pl.ds(TOK, TOK), pl.ds(0, HALF)], core)
    kv_tiles(1)
    pool_block(1)
    p4[...] = pool(p3[...])
    m_y = [send(M_Y + k - 1, p4, ybuf.at[k - 1], ydev[k]) for k in (1, 2, 3)]

    for cp in ld_q:
        cp.wait()

    def q_body(j, _):
        qb[:, lanes(j, 256)] = dot(tok[...], w[:, pl.ds(pl.multiple_of(2 * WID + j * 256, 256), 256)]).astype(BF16)
        return 0

    lax.fori_loop(0, 2, q_body, 0)

    groups = [
        [(0, 256, 0.0), (256, 128, LN2)],
        [(384, 128, 2 * LN2)],
        [(512, 256, None)],
        [(768, 128, None)],
        [(896, 128, None)],
    ]
    chunks = [(gr, first, size) for gr in range(5) for first, size, _ in groups[gr]]
    r_iota = lax.broadcasted_iota(jnp.int32, (256, 256), 0)
    r_level = jnp.where(r_iota < 64, 3, jnp.where(r_iota < 128, 4, 5 + (r_iota // 16) % 2))
    ypb[...] = r_level.astype(F32) * LN2

    def source(first, size, b, h, value):
        col = pl.ds(pl.multiple_of(h * 128 + value * WID, 128), 128)
        if first == 0:
            return kv[pl.ds(b * TOK, TOK), col]
        if first == 256:
            return p0[pl.ds((1 - b) * 128, 128), col]
        return S[pl.ds(first - 384, size), col]

    def score(gr, h, b):
        it = h * 2 + b
        q = qb[pl.ds(b * TOK, TOK), lanes(h, 128)]
        parts = []
        peak = None
        for first, size, bias in groups[gr]:
            l = dot_t(source(first, size, b, h, 0), q) * SCALE
            if bias is None:
                l = l + ypb[pl.ds((first - 512) % 256, size), :]
            elif bias:
                l = l + bias
            parts.append(l)
            top = jnp.max(l, axis=0, keepdims=True)
            peak = top if peak is None else jnp.maximum(peak, top)
        total = None
        for (first, size, _), l in zip(groups[gr], parts):
            e = jnp.exp(l - peak)
            E[it, pl.ds(first, size), :] = e
            part = jnp.sum(e, axis=0, keepdims=True)
            total = part if total is None else total + part
        stat[gr, it, 0:1, :] = peak
        stat[gr, it, 1:2, :] = total

    def each(*steps):
        def body(h, _):
            for b in range(2):
                for f, gr in steps:
                    f(gr, h, b)
            return 0

        lax.fori_loop(0, 4, body, 0)

    for cp in m_y:
        cp.wait_recv()
    wpl[pl.ds(0, 16), :] = ybuf[0]
    wpl[pl.ds(16, 16), :] = pool(jnp.concatenate([ybuf[1], ybuf[2]], axis=0))
    m_x2 = send(M_X2, wpl, rows(S, plane_region(0, 1)), xhi)
    m_zw = [send(M_ZW + k - 1, wpl, rows(S, plane_region(k, 0)), zdev[k]) for k in (1, 2, 3)]
    S[pl.ds(*plane_region(0, 0)), :] = wpl[...]

    def pass_x(b):
        m_x1[b].wait_recv()
        p2x[pl.ds(b * 32, 32), :] = pool(S[pl.ds(b * 64, 64), :])
        p3x[pl.ds(b * 16, 16), :] = pool(p2x[pl.ds(b * 32, 32), :])
        m_zx.extend(pass_z(M_ZX, b, 1, p2x, p3x))

    pass_x(0)
    each((score, 0))
    pass_x(1)
    each((score, 1))
    m_x2.wait_recv()
    s_coth.append(send_cot(1))
    m_zy = [
        send(M_ZY + k - 1, rows(S, plane_region(0, 1)), rows(S, plane_region(k, 1)), zdev[k])
        for k in (1, 2, 3)
    ]

    for cp in m_zo + m_zw:
        cp.wait_recv()
    each((score, 2))

    for cp in m_zx:
        cp.wait_recv()
    each((score, 3))
    for cp in m_zy:
        cp.wait_recv()

    for cp in ld_o:
        cp.wait()

    def finish(h, _):
        for b in range(2):
            it = h * 2 + b
            score(4, h, b)
            peaks = [stat[gr, it, 0:1, :] for gr in range(5)]
            peak = functools.reduce(jnp.maximum, peaks)
            scales = [jnp.exp(m - peak) for m in peaks]
            total = sum(f * stat[gr, it, 1:2, :] for gr, f in enumerate(scales))
            scales = [f / total for f in scales]
            for gr, f in enumerate(scales):
                fin[it, gr : gr + 1, :] = f
            a = None
            for gr, first, size in chunks:
                pb = (E[it, pl.ds(first, size), :] * scales[gr]).astype(BF16)
                part = t_dot(source(first, size, b, h, 1), pb)
                a = part if a is None else a + part
            att[pl.ds(b * TOK, TOK), lanes(h, 128)] = a.T.astype(BF16)
        return 0

    lax.fori_loop(0, 4, finish, 0)

    def cols(i):
        return pl.ds(i * 512, 512)

    def out_piece(i):
        macc[:, cols(i)] = dot(att[pl.ds(0, TOK), :], wo[:, cols(i)])
        c_send[i] = dot(att[pl.ds(TOK, TOK), :], wo[:, cols(i)]).astype(BF16)
        return send(M_MIXC + i, c_send.at[i], c_recv.at[i], core)

    def head_piece(i, cp, total, got, base, src, dst):
        cp.wait_recv()
        src[i] = (total[pl.ds(0, TOK), cols(2 + i)] + got[2 + i].astype(F32)).astype(BF16)
        return send(base + i, src.at[i], dst.at[i], head)

    def last_piece(i, total, got, got_h):
        out_b[:, cols(i)] = (
            total[pl.ds(0, TOK), cols(i)] + got[i].astype(F32) + got_h[i].astype(F32)
        ).astype(BF16)

    s_mixc = {i: out_piece(i) for i in (2, 3, 0, 1)}
    s_mixh = [head_piece(i, s_mixc[2 + i], macc, c_recv, M_MIXH, h_send, h_recv) for i in (0, 1)]

    s_cotf = []
    for i in range(2):
        s_coth[i].wait_recv()
        s_cotf.append(send(
            M_COTF + i, cot.at[COT[i], pl.ds(HALF, HALF)],
            cot.at[pl.ds(TOK + 96 * i, (96, 160)[i]), pl.ds(HALF, HALF)], core,
        ))
    ld_cot.wait()

    def go_tiles(b):
        def body(j, _):
            go[pl.ds(b * TOK, TOK), lanes(j, 256)] = dot_t(
                cot[pl.ds(b * TOK, TOK), :], wo[lanes(j, 256), :]
            ).astype(BF16)
            return 0

        lax.fori_loop(0, 2, body, 0)

    go_tiles(0)
    s_cotc.wait_recv()
    for cp in s_cotf:
        cp.wait_recv()
    go_tiles(1)

    def backward(pair, i):
        h = 2 * pair + i
        hcol = lanes(h, 128)
        vcol = pl.ds(pl.multiple_of(h * 128 + WID, 128), 128)
        for b in range(2):
            q = qb[pl.ds(b * TOK, TOK), hcol]
            g = go[pl.ds(b * TOK, TOK), hcol]
            it = h * 2 + b
            scales = [fin[it, gr : gr + 1, :] for gr in range(5)]
            rd = None
            for gr, first, size in chunks:
                gp = dot_t(source(first, size, b, h, 1), g)
                GP[pl.ds(first, size), :] = gp
                p = E[it, pl.ds(first, size), :] * scales[gr]
                part = jnp.sum(p * gp, axis=0, keepdims=True)
                rd = part if rd is None else rd + part
            dqt = None
            for gr, first, size in chunks:
                p = E[it, pl.ds(first, size), :] * scales[gr]
                dl = (p * (GP[pl.ds(first, size), :] - rd) * SCALE).astype(BF16)
                dvv = dot(p.astype(BF16), g)
                dkk = dot(dl, q)
                part = t_dot(source(first, size, b, h, 0), dl)
                dqt = part if dqt is None else dqt + part
                if first == 0:
                    dkv[pl.ds(b * TOK, TOK), hcol] = dkk
                    dkv[pl.ds(b * TOK, TOK), vcol] = dvv
                elif first == 256:
                    dp0[pl.ds((1 - b) * 128, 128), hcol] = dkk
                    dp0[pl.ds((1 - b) * 128, 128), vcol] = dvv
                elif b == 0:
                    dS[pl.ds(first - 384, size), hcol] = dkk
                    dS[pl.ds(first - 384, size), vcol] = dvv
                else:
                    dkk = dkk + dS[pl.ds(first - 384, size), hcol]
                    dvv = dvv + dS[pl.ds(first - 384, size), vcol]
                    dS[pl.ds(first - 384, size), hcol] = dkk
                    dS[pl.ds(first - 384, size), vcol] = dvv
                    if first > 384:
                        sb[pair, pl.ds(first - 384, size), lanes(i, 128)] = dkk.astype(BF16)
                        sb[pair, pl.ds(first - 384, size), lanes(i + 2, 128)] = dvv.astype(BF16)
            dq[pl.ds(b * TOK, TOK), hcol] = dqt.T.astype(BF16)

    def heads(pair):
        def body(i, _):
            backward(pair, i)
            return 0

        lax.fori_loop(0, 2, body, 0)

    b_z = {0: [], 1: []}

    def send_z(pair, dx):
        for k in (1, 2, 3):
            for base, r in ((B_Z, level_region(k, dx)), (B_ZY, plane_region(k, dx))):
                n = base + 4 * (k - 1) + 2 * dx + pair
                b_z[dx].append(send(n, rows(sb.at[pair], r), rows(RS.at[pair], r), zdev[k]))

    heads(0)
    send_z(0, 1)
    heads(1)
    send_z(1, 1)
    send_z(0, 0)
    send_z(1, 0)

    for b in range(2):
        gk[pl.ds(b * TOK, TOK), :] = (
            spread(dp0[pl.ds(b * 128, 128), :]) + dkv[pl.ds(b * TOK, TOK), :]
        ).astype(BF16)

    def in_early(j, _):
        acc[:, lanes(j, 256)] = dot_t(dq[...], w[lanes(j, 256), pl.ds(2 * WID, WID)]) + dot_t(
            gk[...], w[lanes(j, 256), pl.ds(0, 2 * WID)]
        )
        return 0

    def returned(region):
        a, b = RS[0, pl.ds(*region), :], RS[1, pl.ds(*region), :]
        return jnp.concatenate([a[:, :256], b[:, :256], a[:, 256:], b[:, 256:]], axis=1).astype(F32)

    def collect(dx):
        for cp in b_z[dx]:
            cp.wait_recv()
        low = returned(level_region(2, dx)) + returned(level_region(3, dx))
        top = spread(low) + returned(level_region(1, dx))
        plane = dS[pl.ds(*plane_region(0, dx)), :]
        for k in (1, 2, 3):
            plane = plane + returned(plane_region(k, dx))
        return top, plane

    lax.fori_loop(0, 8, in_early, 0)
    for i in range(4):
        s_mixc[i].wait_send()

    def in_piece(i):
        c_send[i] = acc[pl.ds(TOK, TOK), cols(i)].astype(BF16)
        return send(M_INC + i, c_send.at[i], ic_recv.at[i], core)

    s_inc = {i: in_piece(i) for i in (2, 3, 0, 1)}
    top, plane = collect(1)
    xa_s[pl.ds(0, 128), :] = (spread(top) + dS[pl.ds(0, 128), :]).astype(BF16)
    xa_s[pl.ds(128, 32), :] = plane.astype(BF16)
    b_xa = send(B_XA, xa_s, xa_r, xhi)
    s_inh = [head_piece(i, s_inc[2 + i], acc, ic_recv, M_INH, ih_send, ih_recv) for i in (0, 1)]
    top, plane = collect(0)
    pf[pl.ds(0, 64), :] = top
    pf[pl.ds(64, 32), :] = plane

    b_xa.wait_recv()
    top = pf[pl.ds(0, 64), :]
    plane = pf[pl.ds(64, 32), :] + xa_r[pl.ds(128, 32), :].astype(F32)
    gy_s[0] = plane[0:16].astype(BF16)
    high = spread(plane[16:32])
    gy_s[1] = high[0:16].astype(BF16)
    gy_s[2] = high[16:32].astype(BF16)
    b_y = [send(B_Y + k - 1, gy_s.at[k - 1], gy_r.at[k - 1], ydev[k]) for k in (1, 2, 3)]

    for i in (0, 1):
        s_mixc[i].wait_recv()
        s_mixh[i].wait_recv()
        last_piece(i, macc, c_recv, h_recv)
    st_mix = load(out_b, mix_o)

    for cp in b_y:
        cp.wait_recv()
    g4 = gy_r[0].astype(F32) + gy_r[1].astype(F32) + gy_r[2].astype(F32)
    top = top + spread(spread(g4))
    low = spread(top) + xa_r[pl.ds(0, 128), :].astype(F32)
    low = low.astype(BF16)
    out_i = lax.broadcasted_iota(jnp.int32, (TOK, 64), 0)
    inp_i = lax.broadcasted_iota(jnp.int32, (TOK, 64), 1)
    quarter = jnp.where(out_i // 4 == inp_i, 0.25, 0.0).astype(BF16)

    def late_piece(i):
        late = dot_t(low, w[cols(i), pl.ds(0, 2 * WID)])
        lacc[:, cols(i)] = late[0:64]
        lc_send[i] = late[64:128].astype(BF16)
        return send(M_LC + i, lc_send.at[i], lc_recv.at[i], core)

    def late_head(i):
        s_lc[2 + i].wait_recv()
        lh_send[i] = (lacc[:, cols(2 + i)] + lc_recv[2 + i].astype(F32)).astype(BF16)
        return send(M_LH + i, lh_send.at[i], lh_recv.at[i], head)

    s_lc = {i: late_piece(i) for i in (2, 3)}
    s_lh = [late_head(0)]
    s_lc[0] = late_piece(0)
    s_lh.append(late_head(1))
    s_lc[1] = late_piece(1)
    st_mix.wait()
    for i in (0, 1):
        s_inc[i].wait_recv()
        s_inh[i].wait_recv()
        s_lc[i].wait_recv()
        s_lh[i].wait_recv()
        late = lacc[:, cols(i)] + lc_recv[i].astype(F32) + lh_recv[i].astype(F32)
        out_b[:, cols(i)] = (
            acc[pl.ds(0, TOK), cols(i)] + ic_recv[i].astype(F32) + ih_recv[i].astype(F32)
            + dot(quarter, late.astype(BF16))
        ).astype(BF16)
    st_in = load(out_b, ing_o)

    for i in (0, 1):
        s_mixh[i].wait_send()
    for cp in s_lh + list(s_lc.values()):
        cp.wait_send()
    for cp in s_tok + s_coth + s_cotf + s_inh + list(s_inc.values()) + [s_cotc, m_x2, b_xa]:
        cp.wait_send()
    for cp in m_x1 + m_y + m_zo + m_zw + m_zx + m_zy + b_y + b_z[0] + b_z[1]:
        cp.wait_send()
    st_in.wait()


def copy_out(a, b, a_o, b_o):
    a_o[...] = a[...]
    b_o[...] = b[...]


def per_device(tokens, w_query, w_key, w_value, w_out, cotangent):
    V = pltpu.VMEM
    scratch = [
        V((2 * TOK, 2 * HALF), BF16),
        V((2 * HALF, 3 * WID), BF16),
        V((WID, 2 * HALF), BF16),
        V((2 * TOK, 2 * HALF), BF16),
        V((2 * TOK, 2 * WID), BF16),
        V((2 * TOK, WID), BF16),
        V((2 * TOK, WID), BF16),
        V((256, 2 * WID), BF16),
        V((128, 2 * WID), BF16),
        V((64, 2 * WID), BF16),
        V((32, 2 * WID), BF16),
        V((16, 2 * WID), BF16),
        V((32, 2 * WID), BF16),
        V((64, 2 * WID), BF16),
        V((32, 2 * WID), BF16),
        V((3, 16, 2 * WID), BF16),
        V((ROWS, 2 * WID), BF16),
        V((96, 2 * WID), F32),
        V((8, 1024, 256), F32),
        V((5, 8, 8, 256), F32),
        V((8, 8, 256), F32),
        V((1024, 256), F32),
        V((256, 256), F32),
        V((2 * TOK, WID), BF16),
        V((2 * TOK, 2 * HALF), F32),
        V((TOK, 2 * HALF), F32),
        V((4, TOK, 512), BF16),
        V((4, TOK, 512), BF16),
        V((2, TOK, 512), BF16),
        V((2, TOK, 512), BF16),
        V((4, TOK, 512), BF16),
        V((2, TOK, 512), BF16),
        V((2, TOK, 512), BF16),
        V((64, 2 * HALF), F32),
        V((4, 64, 512), BF16),
        V((4, 64, 512), BF16),
        V((2, 64, 512), BF16),
        V((2, 64, 512), BF16),
        V((2 * TOK, 2 * WID), F32),
        V((256, 2 * WID), F32),
        V((ROWS, 2 * WID), F32),
        V((2, ROWS, WID), BF16),
        V((2, ROWS, WID), BF16),
        V((160, 2 * WID), BF16),
        V((160, 2 * WID), BF16),
        V((3, 16, 2 * WID), BF16),
        V((3, 16, 2 * WID), BF16),
        V((2 * TOK, WID), BF16),
        V((2 * TOK, 2 * WID), BF16),
        V((TOK, HALF), BF16),
        pltpu.SemaphoreType.DMA((16,)),
        pltpu.SemaphoreType.DMA((N_MSG,)),
        pltpu.SemaphoreType.DMA((N_MSG,)),
    ]
    any_spec = pl.BlockSpec(memory_space=pl.ANY)
    out = jax.ShapeDtypeStruct((TOK, HALF), BF16)
    mixed, input_grad = pl.pallas_call(
        kernel,
        out_shape=(out, out),
        in_specs=[any_spec] * 6,
        out_specs=(any_spec, any_spec),
        scratch_shapes=scratch,
        compiler_params=pltpu.CompilerParams(
            collective_id=0, has_side_effects=True, vmem_limit_bytes=60 * 2**20
        ),
    )(tokens, w_query, w_key, w_value, w_out, cotangent)
    return pl.pallas_call(
        copy_out,
        grid=(2,),
        out_shape=(out, out),
        in_specs=[pl.BlockSpec((TOK // 2, HALF), lambda i: (i, 0))] * 2,
        out_specs=[pl.BlockSpec((TOK // 2, HALF), lambda i: (i, 0))] * 2,
    )(mixed, input_grad)


def solution(mesh):
    return jax.shard_map(
        per_device,
        mesh=mesh,
        in_specs=(
            P("seq", None), P(None, "head"), P(None, "head"), P(None, "head"),
            P("head", None), P("seq", "head"),
        ),
        out_specs=(P("seq", "head"), P("seq", "head")),
        check_vma=False,
    )
```

```python
import functools
import math

import jax
import jax.numpy as jnp
from jax import lax
from jax.experimental import pallas as pl
from jax.experimental.pallas import tpu as pltpu
from jax.sharding import PartitionSpec as P

MESH = pl.DeviceIdType.MESH
F32 = jnp.float32
BF16 = jnp.bfloat16
LN2 = math.log(2.0)
SCALE = 1.0 / math.sqrt(128)

TOK = 256
WID = 512
HALF = 1024
ROWS = 640


def level_region(dz, dx):
    return (128 + dx * 256, 64) if dz == 1 else (128 + dx * 256 + 32 * dz, 32)


def half(region, b):
    return (region[0] + b * region[1] // 2, region[1] // 2)


def plane_region(dz, dx):
    return (256 + dx * 256 + 32 * dz, 32)


def dot(a, b):
    return jnp.dot(a, b, preferred_element_type=F32)


def dot_t(a, b):
    return lax.dot_general(a, b, (((1,), (1,)), ((), ())), preferred_element_type=F32)


def pool(value):
    n = value.shape[0]
    out = lax.broadcasted_iota(jnp.int32, (n // 2, n), 0)
    inp = lax.broadcasted_iota(jnp.int32, (n // 2, n), 1)
    return dot(jnp.where(inp // 2 == out, 0.5, 0.0).astype(BF16), value).astype(BF16)


def spread(value):
    n = value.shape[0]
    out = lax.broadcasted_iota(jnp.int32, (2 * n, n), 0)
    inp = lax.broadcasted_iota(jnp.int32, (2 * n, n), 1)
    return dot(jnp.where(out // 2 == inp, 0.5, 0.0).astype(BF16), value.astype(BF16))


def t_dot(a, b):
    return lax.dot_general(a, b, (((0,), (0,)), ((), ())), preferred_element_type=F32)


def lanes(i, width):
    return pl.ds(pl.multiple_of(i * width, width), width)


(
    M_TOK, M_COTC, M_COTH, M_COTF, M_MIXC, M_MIXH, M_INC, M_INH,
    M_Y, M_X1, M_X2, M_ZO, M_ZW, M_ZX, M_ZY,
    B_XA, B_Z, B_ZY, B_Y, M_LC, M_LH, N_MSG,
) = (0, 2, 3, 5, 7, 11, 13, 17, 19, 22, 24, 25, 31, 34, 40, 43, 44, 56, 68, 74, 78, 80)


def kernel(
    tok_h, wq_h, wk_h, wv_h, wo_h, cot_h, mix_o, ing_o,
    tok, w, wo, cot, kv, qb, go, p0, p1, p2, p3, p4, wpl, p2x, p3x, ybuf, S,
    pf, E, stat, fin, GP, ypb, att, acc, macc, c_send, c_recv, h_send, h_recv, ic_recv, ih_send, ih_recv,
    lacc, lc_send, lc_recv, lh_send, lh_recv,
    dkv, dp0, dS, sb, RS, xa_s, xa_r, gy_s, gy_r, dq, gk, out_b,
    lsem, ssem, rsem,
):
    s = lax.axis_index("seq")
    hd = lax.axis_index("head")
    c = s % 2

    def flip(bit):
        return (1 - 2 * ((s // bit) % 2)) * bit

    core = (s + flip(1), hd)
    head = (s, 1 - hd)
    xhi = (s + flip(2), hd)
    zdev = {1: (s + flip(4), hd), 2: (s + flip(8), hd), 3: (s + flip(4) + flip(8), hd)}
    ydev = {1: (s + flip(16), hd), 2: (s + flip(32), hd), 3: (s + flip(16) + flip(32), hd)}

    own = pl.ds(pl.multiple_of(hd * HALF, HALF), HALF)
    oth = pl.ds(pl.multiple_of((1 - hd) * HALF, HALF), HALF)
    wcol = pl.ds(pl.multiple_of(c * WID, WID), WID)
    halves = ((own, pl.ds(0, HALF)), (oth, pl.ds(HALF, HALF)))
    lcount = [0]

    def load(src, dst):
        cp = pltpu.make_async_copy(src, dst, lsem.at[lcount[0]])
        lcount[0] += 1
        cp.start()
        return cp

    ld_tok = [load(tok_h.at[:, a], tok.at[pl.ds(0, TOK), b]) for a, b in halves]
    ld_k = [load(wk_h.at[a, wcol], w.at[b, pl.ds(0, WID)]) for a, b in halves]
    ld_v = [load(wv_h.at[a, wcol], w.at[b, pl.ds(WID, WID)]) for a, b in halves]

    barrier = pltpu.get_barrier_semaphore()
    partners = [core, head, xhi] + [zdev[k] for k in (1, 2, 3)] + [ydev[k] for k in (1, 2, 3)]
    for d in partners:
        pl.semaphore_signal(barrier, inc=1, device_id=d, device_id_type=MESH)
    pl.semaphore_wait(barrier, len(partners))

    def send(n, src, dst, dev):
        cp = pltpu.make_async_remote_copy(
            src_ref=src, dst_ref=dst, send_sem=ssem.at[n], recv_sem=rsem.at[n],
            device_id=dev, device_id_type=MESH,
        )
        cp.start()
        return cp

    def rows(ref, region):
        return ref.at[pl.ds(*region)]

    s_tok = [
        send(M_TOK + i, tok_h.at[:, a], tok.at[pl.ds(TOK, TOK), b], core)
        for i, (a, b) in enumerate(halves)
    ]
    COT = [pl.ds(0, 96), pl.ds(96, 160)]

    def send_cot(i):
        part = COT[i]
        return send(M_COTH + i, cot_h.at[part], cot.at[part, pl.ds(HALF, HALF)], head)

    s_coth = [send_cot(0)]

    for cp in ld_tok + ld_k + ld_v:
        cp.wait()
    ld_q = [load(wq_h.at[a, wcol], w.at[b, pl.ds(2 * WID, WID)]) for a, b in halves]
    ld_cot = load(cot_h, cot.at[pl.ds(0, TOK), pl.ds(0, HALF)])
    ld_o = [load(wo_h.at[wcol, a], wo.at[:, b]) for a, b in halves]

    def kv_tiles(b):
        def body(j, _):
            r = dot(tok[pl.ds(b * TOK, TOK), :], w[:, lanes(j, 256)]).astype(BF16)
            kv[pl.ds(b * TOK, TOK), lanes(j, 256)] = r
            return 0

        lax.fori_loop(0, 4, body, 0)

    m_x1, m_zo, m_zx = [], [], []

    def pool_block(b):
        p0[pl.ds(b * 128, 128), :] = pool(kv[pl.ds(b * TOK, TOK), :])
        p1[pl.ds(b * 64, 64), :] = pool(p0[pl.ds(b * 128, 128), :])
        m_x1.append(send(M_X1 + b, rows(p1, (b * 64, 64)), rows(S, (b * 64, 64)), xhi))
        p2[pl.ds(b * 32, 32), :] = pool(p1[pl.ds(b * 64, 64), :])
        p3[pl.ds(b * 16, 16), :] = pool(p2[pl.ds(b * 32, 32), :])
        m_zo.extend(pass_z(M_ZO, b, 0, p2, p3))

    def pass_z(base, b, dx, two, three):
        out = []
        for k in (1, 2, 3):
            src = rows(two, (b * 32, 32)) if k == 1 else rows(three, (b * 16, 16))
            out.append(send(base + 2 * (k - 1) + b, src, rows(S, half(level_region(k, dx), b)), zdev[k]))
        return out

    kv_tiles(0)
    pool_block(0)
    for cp in s_tok:
        cp.wait_recv()
    s_cotc = send(M_COTC, cot_h, cot.at[pl.ds(TOK, TOK), pl.ds(0, HALF)], core)
    kv_tiles(1)
    pool_block(1)
    p4[...] = pool(p3[...])
    m_y = [send(M_Y + k - 1, p4, ybuf.at[k - 1], ydev[k]) for k in (1, 2, 3)]

    for cp in ld_q:
        cp.wait()

    def q_body(j, _):
        qb[:, lanes(j, 256)] = dot(tok[...], w[:, pl.ds(pl.multiple_of(2 * WID + j * 256, 256), 256)]).astype(BF16)
        return 0

    lax.fori_loop(0, 2, q_body, 0)

    groups = [
        [(0, 256, 0.0), (256, 128, LN2)],
        [(384, 128, 2 * LN2)],
        [(512, 256, None)],
        [(768, 128, None)],
        [(896, 128, None)],
    ]
    chunks = [(gr, first, size) for gr in range(5) for first, size, _ in groups[gr]]
    r_iota = lax.broadcasted_iota(jnp.int32, (256, 256), 0)
    r_level = jnp.where(r_iota < 64, 3, jnp.where(r_iota < 128, 4, 5 + (r_iota // 16) % 2))
    ypb[...] = r_level.astype(F32) * LN2

    def source(first, size, b, h, value):
        col = pl.ds(pl.multiple_of(h * 128 + value * WID, 128), 128)
        if first == 0:
            return kv[pl.ds(b * TOK, TOK), col]
        if first == 256:
            return p0[pl.ds((1 - b) * 128, 128), col]
        return S[pl.ds(first - 384, size), col]

    def score(gr, h, b):
        it = h * 2 + b
        q = qb[pl.ds(b * TOK, TOK), lanes(h, 128)]
        parts = []
        peak = None
        for first, size, bias in groups[gr]:
            l = dot_t(source(first, size, b, h, 0), q) * SCALE
            if bias is None:
                l = l + ypb[pl.ds((first - 512) % 256, size), :]
            elif bias:
                l = l + bias
            parts.append(l)
            top = jnp.max(l, axis=0, keepdims=True)
            peak = top if peak is None else jnp.maximum(peak, top)
        total = None
        for (first, size, _), l in zip(groups[gr], parts):
            e = jnp.exp(l - peak)
            E[it, pl.ds(first, size), :] = e
            part = jnp.sum(e, axis=0, keepdims=True)
            total = part if total is None else total + part
        stat[gr, it, 0:1, :] = peak
        stat[gr, it, 1:2, :] = total

    def each(*steps):
        def body(h, _):
            for b in range(2):
                for f, gr in steps:
                    f(gr, h, b)
            return 0

        lax.fori_loop(0, 4, body, 0)

    for cp in m_y:
        cp.wait_recv()
    wpl[pl.ds(0, 16), :] = ybuf[0]
    wpl[pl.ds(16, 16), :] = pool(jnp.concatenate([ybuf[1], ybuf[2]], axis=0))
    m_x2 = send(M_X2, wpl, rows(S, plane_region(0, 1)), xhi)
    m_zw = [send(M_ZW + k - 1, wpl, rows(S, plane_region(k, 0)), zdev[k]) for k in (1, 2, 3)]
    S[pl.ds(*plane_region(0, 0)), :] = wpl[...]

    def pass_x(b):
        m_x1[b].wait_recv()
        p2x[pl.ds(b * 32, 32), :] = pool(S[pl.ds(b * 64, 64), :])
        p3x[pl.ds(b * 16, 16), :] = pool(p2x[pl.ds(b * 32, 32), :])
        m_zx.extend(pass_z(M_ZX, b, 1, p2x, p3x))

    pass_x(0)
    each((score, 0))
    pass_x(1)
    each((score, 1))
    m_x2.wait_recv()
    s_coth.append(send_cot(1))
    m_zy = [
        send(M_ZY + k - 1, rows(S, plane_region(0, 1)), rows(S, plane_region(k, 1)), zdev[k])
        for k in (1, 2, 3)
    ]

    for cp in m_zo + m_zw:
        cp.wait_recv()
    each((score, 2))

    for cp in m_zx:
        cp.wait_recv()
    each((score, 3))
    for cp in m_zy:
        cp.wait_recv()

    for cp in ld_o:
        cp.wait()

    def finish(h, _):
        for b in range(2):
            it = h * 2 + b
            score(4, h, b)
            peaks = [stat[gr, it, 0:1, :] for gr in range(5)]
            peak = functools.reduce(jnp.maximum, peaks)
            scales = [jnp.exp(m - peak) for m in peaks]
            total = sum(f * stat[gr, it, 1:2, :] for gr, f in enumerate(scales))
            scales = [f / total for f in scales]
            for gr, f in enumerate(scales):
                fin[it, gr : gr + 1, :] = f
            a = None
            for gr, first, size in chunks:
                pb = (E[it, pl.ds(first, size), :] * scales[gr]).astype(BF16)
                part = t_dot(source(first, size, b, h, 1), pb)
                a = part if a is None else a + part
            att[pl.ds(b * TOK, TOK), lanes(h, 128)] = a.T.astype(BF16)
        return 0

    lax.fori_loop(0, 4, finish, 0)

    def cols(i):
        return pl.ds(i * 512, 512)

    def out_piece(i):
        macc[:, cols(i)] = dot(att[pl.ds(0, TOK), :], wo[:, cols(i)])
        c_send[i] = dot(att[pl.ds(TOK, TOK), :], wo[:, cols(i)]).astype(BF16)
        return send(M_MIXC + i, c_send.at[i], c_recv.at[i], core)

    def head_piece(i, cp, total, got, base, src, dst):
        cp.wait_recv()
        src[i] = (total[pl.ds(0, TOK), cols(2 + i)] + got[2 + i].astype(F32)).astype(BF16)
        return send(base + i, src.at[i], dst.at[i], head)

    def last_piece(i, total, got, got_h):
        out_b[:, cols(i)] = (
            total[pl.ds(0, TOK), cols(i)] + got[i].astype(F32) + got_h[i].astype(F32)
        ).astype(BF16)

    s_mixc = {i: out_piece(i) for i in (2, 3, 0, 1)}
    s_mixh = [head_piece(i, s_mixc[2 + i], macc, c_recv, M_MIXH, h_send, h_recv) for i in (0, 1)]

    s_cotf = []
    for i in range(2):
        s_coth[i].wait_recv()
        s_cotf.append(send(
            M_COTF + i, cot.at[COT[i], pl.ds(HALF, HALF)],
            cot.at[pl.ds(TOK + 96 * i, (96, 160)[i]), pl.ds(HALF, HALF)], core,
        ))
    ld_cot.wait()

    def go_tiles(b):
        def body(j, _):
            go[pl.ds(b * TOK, TOK), lanes(j, 256)] = dot_t(
                cot[pl.ds(b * TOK, TOK), :], wo[lanes(j, 256), :]
            ).astype(BF16)
            return 0

        lax.fori_loop(0, 2, body, 0)

    go_tiles(0)
    s_cotc.wait_recv()
    for cp in s_cotf:
        cp.wait_recv()
    go_tiles(1)

    def backward(pair, i):
        h = 2 * pair + i
        hcol = lanes(h, 128)
        vcol = pl.ds(pl.multiple_of(h * 128 + WID, 128), 128)
        for b in range(2):
            q = qb[pl.ds(b * TOK, TOK), hcol]
            g = go[pl.ds(b * TOK, TOK), hcol]
            it = h * 2 + b
            scales = [fin[it, gr : gr + 1, :] for gr in range(5)]
            rd = None
            for gr, first, size in chunks:
                gp = dot_t(source(first, size, b, h, 1), g)
                GP[pl.ds(first, size), :] = gp
                p = E[it, pl.ds(first, size), :] * scales[gr]
                part = jnp.sum(p * gp, axis=0, keepdims=True)
                rd = part if rd is None else rd + part
            dqt = None
            for gr, first, size in chunks:
                p = E[it, pl.ds(first, size), :] * scales[gr]
                dl = (p * (GP[pl.ds(first, size), :] - rd) * SCALE).astype(BF16)
                dvv = dot(p.astype(BF16), g)
                dkk = dot(dl, q)
                part = t_dot(source(first, size, b, h, 0), dl)
                dqt = part if dqt is None else dqt + part
                if first == 0:
                    dkv[pl.ds(b * TOK, TOK), hcol] = dkk
                    dkv[pl.ds(b * TOK, TOK), vcol] = dvv
                elif first == 256:
                    dp0[pl.ds((1 - b) * 128, 128), hcol] = dkk
                    dp0[pl.ds((1 - b) * 128, 128), vcol] = dvv
                elif b == 0:
                    dS[pl.ds(first - 384, size), hcol] = dkk
                    dS[pl.ds(first - 384, size), vcol] = dvv
                else:
                    dkk = dkk + dS[pl.ds(first - 384, size), hcol]
                    dvv = dvv + dS[pl.ds(first - 384, size), vcol]
                    dS[pl.ds(first - 384, size), hcol] = dkk
                    dS[pl.ds(first - 384, size), vcol] = dvv
                    if first > 384:
                        sb[pair, pl.ds(first - 384, size), lanes(i, 128)] = dkk.astype(BF16)
                        sb[pair, pl.ds(first - 384, size), lanes(i + 2, 128)] = dvv.astype(BF16)
            dq[pl.ds(b * TOK, TOK), hcol] = dqt.T.astype(BF16)

    def heads(pair):
        def body(i, _):
            backward(pair, i)
            return 0

        lax.fori_loop(0, 2, body, 0)

    b_z = {0: [], 1: []}

    def send_z(pair, dx):
        for k in (1, 2, 3):
            for base, r in ((B_Z, level_region(k, dx)), (B_ZY, plane_region(k, dx))):
                n = base + 4 * (k - 1) + 2 * dx + pair
                b_z[dx].append(send(n, rows(sb.at[pair], r), rows(RS.at[pair], r), zdev[k]))

    heads(0)
    send_z(0, 1)
    heads(1)
    send_z(1, 1)
    send_z(0, 0)
    send_z(1, 0)

    for b in range(2):
        gk[pl.ds(b * TOK, TOK), :] = (
            spread(dp0[pl.ds(b * 128, 128), :]) + dkv[pl.ds(b * TOK, TOK), :]
        ).astype(BF16)

    def in_early(j, _):
        acc[:, lanes(j, 256)] = dot_t(dq[...], w[lanes(j, 256), pl.ds(2 * WID, WID)]) + dot_t(
            gk[...], w[lanes(j, 256), pl.ds(0, 2 * WID)]
        )
        return 0

    def returned(region):
        a, b = RS[0, pl.ds(*region), :], RS[1, pl.ds(*region), :]
        return jnp.concatenate([a[:, :256], b[:, :256], a[:, 256:], b[:, 256:]], axis=1).astype(F32)

    def collect(dx):
        for cp in b_z[dx]:
            cp.wait_recv()
        low = returned(level_region(2, dx)) + returned(level_region(3, dx))
        top = spread(low) + returned(level_region(1, dx))
        plane = dS[pl.ds(*plane_region(0, dx)), :]
        for k in (1, 2, 3):
            plane = plane + returned(plane_region(k, dx))
        return top, plane

    for i in range(4):
        s_mixc[i].wait_send()

    def in_piece(i):
        lax.fori_loop(2 * i, 2 * i + 2, in_early, 0)
        c_send[i] = acc[pl.ds(TOK, TOK), cols(i)].astype(BF16)
        return send(M_INC + i, c_send.at[i], ic_recv.at[i], core)

    def early_piece(i):
        return head_piece(i, s_inc[2 + i], acc, ic_recv, M_INH, ih_send, ih_recv)

    s_inc = {i: in_piece(i) for i in (2, 3)}
    s_inh = [early_piece(0)]

    def send_y(dx, plane):
        gy_s[dx, 0] = plane[0:16].astype(BF16)
        high = spread(plane[16:32])
        gy_s[dx, 1] = high[0:16].astype(BF16)
        gy_s[dx, 2] = high[16:32].astype(BF16)
        return [
            send(B_Y + 3 * dx + k - 1, gy_s.at[dx, k - 1], gy_r.at[dx, k - 1], ydev[k]) for k in (1, 2, 3)
        ]

    def add_y(dx, top):
        for cp in b_y[dx]:
            cp.wait_recv()
        g4 = gy_r[dx, 0].astype(F32) + gy_r[dx, 1].astype(F32) + gy_r[dx, 2].astype(F32)
        return top + spread(spread(g4))

    b_y = {}
    top, plane = collect(1)
    b_y[1] = send_y(1, plane)
    pf[pl.ds(0, 64), :] = top
    top = add_y(1, pf[pl.ds(0, 64), :])
    xa_s[...] = (spread(top) + dS[pl.ds(0, 128), :]).astype(BF16)
    b_xa = send(B_XA, xa_s, xa_r, xhi)
    s_inh.append(early_piece(1))
    s_inc.update({i: in_piece(i) for i in (0, 1)})
    top, plane = collect(0)
    b_y[0] = send_y(0, plane)
    pf[pl.ds(64, 64), :] = top

    for i in (0, 1):
        s_mixc[i].wait_recv()
        s_mixh[i].wait_recv()
        last_piece(i, macc, c_recv, h_recv)
    st_mix = load(out_b, mix_o)

    low = spread(add_y(0, pf[pl.ds(64, 64), :]))
    b_xa.wait_recv()
    low = low + xa_r[...].astype(F32)
    low = low.astype(BF16)
    out_i = lax.broadcasted_iota(jnp.int32, (TOK, 64), 0)
    inp_i = lax.broadcasted_iota(jnp.int32, (TOK, 64), 1)
    quarter = jnp.where(out_i // 4 == inp_i, 0.25, 0.0).astype(BF16)

    def late_piece(i):
        late = dot_t(low, w[cols(i), pl.ds(0, 2 * WID)])
        lacc[:, cols(i)] = late[0:64]
        lc_send[i] = late[64:128].astype(BF16)
        return send(M_LC + i, lc_send.at[i], lc_recv.at[i], core)

    def late_head(i):
        s_lc[2 + i].wait_recv()
        lh_send[i] = (lacc[:, cols(2 + i)] + lc_recv[2 + i].astype(F32)).astype(BF16)
        return send(M_LH + i, lh_send.at[i], lh_recv.at[i], head)

    s_lc = {i: late_piece(i) for i in (2, 3)}
    s_lh = [late_head(0)]
    s_lc[0] = late_piece(0)
    s_lh.append(late_head(1))
    s_lc[1] = late_piece(1)
    st_mix.wait()
    for i in (0, 1):
        s_inc[i].wait_recv()
        s_inh[i].wait_recv()
        s_lc[i].wait_recv()
        s_lh[i].wait_recv()
        late = lacc[:, cols(i)] + lc_recv[i].astype(F32) + lh_recv[i].astype(F32)
        out_b[:, cols(i)] = (
            acc[pl.ds(0, TOK), cols(i)] + ic_recv[i].astype(F32) + ih_recv[i].astype(F32)
            + dot(quarter, late.astype(BF16))
        ).astype(BF16)
    st_in = load(out_b, ing_o)

    for i in (0, 1):
        s_mixh[i].wait_send()
    for cp in s_lh + list(s_lc.values()):
        cp.wait_send()
    for cp in s_tok + s_coth + s_cotf + s_inh + list(s_inc.values()) + [s_cotc, m_x2, b_xa]:
        cp.wait_send()
    for cp in m_x1 + m_y + m_zo + m_zw + m_zx + m_zy + b_y[0] + b_y[1] + b_z[0] + b_z[1]:
        cp.wait_send()
    st_in.wait()


def copy_out(a, b, a_o, b_o):
    a_o[...] = a[...]
    b_o[...] = b[...]


def per_device(tokens, w_query, w_key, w_value, w_out, cotangent):
    V = pltpu.VMEM
    scratch = [
        V((2 * TOK, 2 * HALF), BF16),
        V((2 * HALF, 3 * WID), BF16),
        V((WID, 2 * HALF), BF16),
        V((2 * TOK, 2 * HALF), BF16),
        V((2 * TOK, 2 * WID), BF16),
        V((2 * TOK, WID), BF16),
        V((2 * TOK, WID), BF16),
        V((256, 2 * WID), BF16),
        V((128, 2 * WID), BF16),
        V((64, 2 * WID), BF16),
        V((32, 2 * WID), BF16),
        V((16, 2 * WID), BF16),
        V((32, 2 * WID), BF16),
        V((64, 2 * WID), BF16),
        V((32, 2 * WID), BF16),
        V((3, 16, 2 * WID), BF16),
        V((ROWS, 2 * WID), BF16),
        V((128, 2 * WID), F32),
        V((8, 1024, 256), F32),
        V((5, 8, 8, 256), F32),
        V((8, 8, 256), F32),
        V((1024, 256), F32),
        V((256, 256), F32),
        V((2 * TOK, WID), BF16),
        V((2 * TOK, 2 * HALF), F32),
        V((TOK, 2 * HALF), F32),
        V((4, TOK, 512), BF16),
        V((4, TOK, 512), BF16),
        V((2, TOK, 512), BF16),
        V((2, TOK, 512), BF16),
        V((4, TOK, 512), BF16),
        V((2, TOK, 512), BF16),
        V((2, TOK, 512), BF16),
        V((64, 2 * HALF), F32),
        V((4, 64, 512), BF16),
        V((4, 64, 512), BF16),
        V((2, 64, 512), BF16),
        V((2, 64, 512), BF16),
        V((2 * TOK, 2 * WID), F32),
        V((256, 2 * WID), F32),
        V((ROWS, 2 * WID), F32),
        V((2, ROWS, WID), BF16),
        V((2, ROWS, WID), BF16),
        V((128, 2 * WID), BF16),
        V((128, 2 * WID), BF16),
        V((2, 3, 16, 2 * WID), BF16),
        V((2, 3, 16, 2 * WID), BF16),
        V((2 * TOK, WID), BF16),
        V((2 * TOK, 2 * WID), BF16),
        V((TOK, HALF), BF16),
        pltpu.SemaphoreType.DMA((16,)),
        pltpu.SemaphoreType.DMA((N_MSG,)),
        pltpu.SemaphoreType.DMA((N_MSG,)),
    ]
    any_spec = pl.BlockSpec(memory_space=pl.ANY)
    out = jax.ShapeDtypeStruct((TOK, HALF), BF16)
    mixed, input_grad = pl.pallas_call(
        kernel,
        out_shape=(out, out),
        in_specs=[any_spec] * 6,
        out_specs=(any_spec, any_spec),
        scratch_shapes=scratch,
        compiler_params=pltpu.CompilerParams(
            collective_id=0, has_side_effects=True, vmem_limit_bytes=60 * 2**20
        ),
    )(tokens, w_query, w_key, w_value, w_out, cotangent)
    return pl.pallas_call(
        copy_out,
        grid=(2,),
        out_shape=(out, out),
        in_specs=[pl.BlockSpec((TOK // 2, HALF), lambda i: (i, 0))] * 2,
        out_specs=[pl.BlockSpec((TOK // 2, HALF), lambda i: (i, 0))] * 2,
    )(mixed, input_grad)


def solution(mesh):
    return jax.shard_map(
        per_device,
        mesh=mesh,
        in_specs=(
            P("seq", None), P(None, "head"), P(None, "head"), P(None, "head"),
            P("head", None), P("seq", "head"),
        ),
        out_specs=(P("seq", "head"), P("seq", "head")),
        check_vma=False,
    )
```

```python
import functools
import math

import jax
import jax.numpy as jnp
from jax import lax
from jax.experimental import pallas as pl
from jax.experimental.pallas import tpu as pltpu
from jax.sharding import PartitionSpec as P

MESH = pl.DeviceIdType.MESH
F32 = jnp.float32
BF16 = jnp.bfloat16
LN2 = math.log(2.0)
SCALE = 1.0 / math.sqrt(128)

TOK = 256
WID = 512
HALF = 1024
ROWS = 640


def level_region(dz, dx):
    return (128 + dx * 256, 64) if dz == 1 else (128 + dx * 256 + 32 * dz, 32)


def half(region, b):
    return (region[0] + b * region[1] // 2, region[1] // 2)


def plane_region(dz, dx):
    return (256 + dx * 256 + 32 * dz, 32)


def dot(a, b):
    return jnp.dot(a, b, preferred_element_type=F32)


def dot_t(a, b):
    return lax.dot_general(a, b, (((1,), (1,)), ((), ())), preferred_element_type=F32)


def pool(value):
    n = value.shape[0]
    out = lax.broadcasted_iota(jnp.int32, (n // 2, n), 0)
    inp = lax.broadcasted_iota(jnp.int32, (n // 2, n), 1)
    return dot(jnp.where(inp // 2 == out, 0.5, 0.0).astype(BF16), value).astype(BF16)


def spread(value):
    n = value.shape[0]
    out = lax.broadcasted_iota(jnp.int32, (2 * n, n), 0)
    inp = lax.broadcasted_iota(jnp.int32, (2 * n, n), 1)
    return dot(jnp.where(out // 2 == inp, 0.5, 0.0).astype(BF16), value.astype(BF16))


def t_dot(a, b):
    return lax.dot_general(a, b, (((0,), (0,)), ((), ())), preferred_element_type=F32)


def lanes(i, width):
    return pl.ds(pl.multiple_of(i * width, width), width)


(
    M_TOK, M_COTC, M_COTH, M_COTF, M_MIXC, M_MIXH, M_INC, M_INH,
    M_Y, M_X1, M_X2, M_ZO, M_ZW, M_ZX, M_ZY,
    B_XA, B_Z, B_ZY, B_Y, M_LC, M_LH, N_MSG,
) = (0, 2, 3, 5, 7, 11, 13, 17, 19, 22, 24, 25, 31, 34, 40, 43, 44, 56, 68, 74, 78, 80)


def kernel(
    tok_h, wq_h, wk_h, wv_h, wo_h, cot_h, mix_o, ing_o,
    tok, w, wo, cot, kv, qb, go, p0, p1, p2, p3, p4, wpl, p2x, p3x, ybuf, S,
    pf, E, stat, fin, GP, ypb, att, acc, macc, c_send, c_recv, h_send, h_recv, ic_recv, ih_send, ih_recv,
    lacc, lc_send, lc_recv, lh_send, lh_recv,
    dkv, dp0, dS, sb, RS, xa_s, xa_r, gy_s, gy_r, dq, gk, out_b,
    lsem, ssem, rsem,
):
    s = lax.axis_index("seq")
    hd = lax.axis_index("head")
    c = s % 2

    def flip(bit):
        return (1 - 2 * ((s // bit) % 2)) * bit

    core = (s + flip(1), hd)
    head = (s, 1 - hd)
    xhi = (s + flip(2), hd)
    zdev = {1: (s + flip(4), hd), 2: (s + flip(8), hd), 3: (s + flip(4) + flip(8), hd)}
    ydev = {1: (s + flip(16), hd), 2: (s + flip(32), hd), 3: (s + flip(16) + flip(32), hd)}

    own = pl.ds(pl.multiple_of(hd * HALF, HALF), HALF)
    oth = pl.ds(pl.multiple_of((1 - hd) * HALF, HALF), HALF)
    wcol = pl.ds(pl.multiple_of(c * WID, WID), WID)
    halves = ((own, pl.ds(0, HALF)), (oth, pl.ds(HALF, HALF)))
    lcount = [0]

    def load(src, dst):
        cp = pltpu.make_async_copy(src, dst, lsem.at[lcount[0]])
        lcount[0] += 1
        cp.start()
        return cp

    ld_tok = [load(tok_h.at[:, a], tok.at[pl.ds(0, TOK), b]) for a, b in halves]
    ld_k = [load(wk_h.at[a, wcol], w.at[b, pl.ds(0, WID)]) for a, b in halves]
    ld_v = [load(wv_h.at[a, wcol], w.at[b, pl.ds(WID, WID)]) for a, b in halves]

    barrier = pltpu.get_barrier_semaphore()
    partners = [core, head, xhi] + [zdev[k] for k in (1, 2, 3)] + [ydev[k] for k in (1, 2, 3)]
    for d in partners:
        pl.semaphore_signal(barrier, inc=1, device_id=d, device_id_type=MESH)
    pl.semaphore_wait(barrier, len(partners))

    def send(n, src, dst, dev):
        cp = pltpu.make_async_remote_copy(
            src_ref=src, dst_ref=dst, send_sem=ssem.at[n], recv_sem=rsem.at[n],
            device_id=dev, device_id_type=MESH,
        )
        cp.start()
        return cp

    def rows(ref, region):
        return ref.at[pl.ds(*region)]

    s_tok = [
        send(M_TOK + i, tok_h.at[:, a], tok.at[pl.ds(TOK, TOK), b], core)
        for i, (a, b) in enumerate(halves)
    ]
    COT = [pl.ds(0, 96), pl.ds(96, 160)]

    def send_cot(i):
        part = COT[i]
        return send(M_COTH + i, cot_h.at[part], cot.at[part, pl.ds(HALF, HALF)], head)

    s_coth = [send_cot(0)]

    for cp in ld_tok + ld_k + ld_v:
        cp.wait()
    ld_q = [load(wq_h.at[a, wcol], w.at[b, pl.ds(2 * WID, WID)]) for a, b in halves]
    ld_cot = load(cot_h, cot.at[pl.ds(0, TOK), pl.ds(0, HALF)])
    ld_o = [load(wo_h.at[wcol, a], wo.at[:, b]) for a, b in halves]

    def kv_tiles(b):
        def body(j, _):
            r = dot(tok[pl.ds(b * TOK, TOK), :], w[:, lanes(j, 512)]).astype(BF16)
            kv[pl.ds(b * TOK, TOK), lanes(j, 512)] = r
            return 0

        lax.fori_loop(0, 2, body, 0)

    m_x1, m_zo, m_zx = [], [], []

    def pool_block(b):
        p0[pl.ds(b * 128, 128), :] = pool(kv[pl.ds(b * TOK, TOK), :])
        p1[pl.ds(b * 64, 64), :] = pool(p0[pl.ds(b * 128, 128), :])
        m_x1.append(send(M_X1 + b, rows(p1, (b * 64, 64)), rows(S, (b * 64, 64)), xhi))
        p2[pl.ds(b * 32, 32), :] = pool(p1[pl.ds(b * 64, 64), :])
        p3[pl.ds(b * 16, 16), :] = pool(p2[pl.ds(b * 32, 32), :])
        m_zo.extend(pass_z(M_ZO, b, 0, p2, p3))

    def pass_z(base, b, dx, two, three):
        out = []
        for k in (1, 2, 3):
            src = rows(two, (b * 32, 32)) if k == 1 else rows(three, (b * 16, 16))
            out.append(send(base + 2 * (k - 1) + b, src, rows(S, half(level_region(k, dx), b)), zdev[k]))
        return out

    kv_tiles(0)
    pool_block(0)
    for cp in s_tok:
        cp.wait_recv()
    s_cotc = send(M_COTC, cot_h, cot.at[pl.ds(TOK, TOK), pl.ds(0, HALF)], core)
    kv_tiles(1)
    pool_block(1)
    p4[...] = pool(p3[...])
    m_y = [send(M_Y + k - 1, p4, ybuf.at[k - 1], ydev[k]) for k in (1, 2, 3)]

    for cp in ld_q:
        cp.wait()

    def q_body(j, _):
        qb[:, lanes(j, 256)] = dot(tok[...], w[:, pl.ds(pl.multiple_of(2 * WID + j * 256, 256), 256)]).astype(BF16)
        return 0

    lax.fori_loop(0, 2, q_body, 0)

    groups = [
        [(0, 256, 0.0), (256, 128, LN2)],
        [(384, 128, 2 * LN2)],
        [(512, 256, None)],
        [(768, 128, None)],
        [(896, 128, None)],
    ]
    chunks = [(gr, first, size) for gr in range(5) for first, size, _ in groups[gr]]
    r_iota = lax.broadcasted_iota(jnp.int32, (256, 256), 0)
    r_level = jnp.where(r_iota < 64, 3, jnp.where(r_iota < 128, 4, 5 + (r_iota // 16) % 2))
    ypb[...] = r_level.astype(F32) * LN2

    def source(first, size, b, h, value):
        col = pl.ds(pl.multiple_of(h * 128 + value * WID, 128), 128)
        if first == 0:
            return kv[pl.ds(b * TOK, TOK), col]
        if first == 256:
            return p0[pl.ds((1 - b) * 128, 128), col]
        return S[pl.ds(first - 384, size), col]

    def score(gr, h, b):
        it = h * 2 + b
        q = qb[pl.ds(b * TOK, TOK), lanes(h, 128)]
        parts = []
        peak = None
        for first, size, bias in groups[gr]:
            l = dot_t(source(first, size, b, h, 0), q) * SCALE
            if bias is None:
                l = l + ypb[pl.ds((first - 512) % 256, size), :]
            elif bias:
                l = l + bias
            parts.append(l)
            top = jnp.max(l, axis=0, keepdims=True)
            peak = top if peak is None else jnp.maximum(peak, top)
        total = None
        for (first, size, _), l in zip(groups[gr], parts):
            e = jnp.exp(l - peak)
            E[it, pl.ds(first, size), :] = e
            part = jnp.sum(e, axis=0, keepdims=True)
            total = part if total is None else total + part
        stat[gr, it, 0:1, :] = peak
        stat[gr, it, 1:2, :] = total

    def each(*steps):
        def body(h, _):
            for b in range(2):
                for f, gr in steps:
                    f(gr, h, b)
            return 0

        lax.fori_loop(0, 4, body, 0)

    for cp in m_y:
        cp.wait_recv()
    wpl[pl.ds(0, 16), :] = ybuf[0]
    wpl[pl.ds(16, 16), :] = pool(jnp.concatenate([ybuf[1], ybuf[2]], axis=0))
    m_x2 = send(M_X2, wpl, rows(S, plane_region(0, 1)), xhi)
    m_zw = [send(M_ZW + k - 1, wpl, rows(S, plane_region(k, 0)), zdev[k]) for k in (1, 2, 3)]
    S[pl.ds(*plane_region(0, 0)), :] = wpl[...]

    def pass_x(b):
        m_x1[b].wait_recv()
        p2x[pl.ds(b * 32, 32), :] = pool(S[pl.ds(b * 64, 64), :])
        p3x[pl.ds(b * 16, 16), :] = pool(p2x[pl.ds(b * 32, 32), :])
        m_zx.extend(pass_z(M_ZX, b, 1, p2x, p3x))

    pass_x(0)
    each((score, 0))
    pass_x(1)
    m_x2.wait_recv()
    s_coth.append(send_cot(1))
    m_zy = [
        send(M_ZY + k - 1, rows(S, plane_region(0, 1)), rows(S, plane_region(k, 1)), zdev[k])
        for k in (1, 2, 3)
    ]

    for cp in m_zo + m_zw:
        cp.wait_recv()
    each((score, 1), (score, 2))

    for cp in m_zx:
        cp.wait_recv()
    each((score, 3))
    for cp in m_zy:
        cp.wait_recv()

    for cp in ld_o:
        cp.wait()

    def finish(h, _):
        for b in range(2):
            it = h * 2 + b
            score(4, h, b)
            peaks = [stat[gr, it, 0:1, :] for gr in range(5)]
            peak = functools.reduce(jnp.maximum, peaks)
            scales = [jnp.exp(m - peak) for m in peaks]
            total = sum(f * stat[gr, it, 1:2, :] for gr, f in enumerate(scales))
            scales = [f / total for f in scales]
            for gr, f in enumerate(scales):
                fin[it, gr : gr + 1, :] = f
            a = None
            for gr, first, size in chunks:
                pb = (E[it, pl.ds(first, size), :] * scales[gr]).astype(BF16)
                part = t_dot(source(first, size, b, h, 1), pb)
                a = part if a is None else a + part
            att[pl.ds(b * TOK, TOK), lanes(h, 128)] = a.T.astype(BF16)
        return 0

    lax.fori_loop(0, 4, finish, 0)

    def cols(i):
        return pl.ds(i * 512, 512)

    def out_piece(i):
        macc[:, cols(i)] = dot(att[pl.ds(0, TOK), :], wo[:, cols(i)])
        c_send[i] = dot(att[pl.ds(TOK, TOK), :], wo[:, cols(i)]).astype(BF16)
        return send(M_MIXC + i, c_send.at[i], c_recv.at[i], core)

    def head_piece(i, cp, total, got, base, src, dst):
        cp.wait_recv()
        src[i] = (total[pl.ds(0, TOK), cols(2 + i)] + got[2 + i].astype(F32)).astype(BF16)
        return send(base + i, src.at[i], dst.at[i], head)

    def last_piece(i, total, got, got_h):
        out_b[:, cols(i)] = (
            total[pl.ds(0, TOK), cols(i)] + got[i].astype(F32) + got_h[i].astype(F32)
        ).astype(BF16)

    s_mixc = {i: out_piece(i) for i in (2, 3, 0, 1)}
    s_mixh = [head_piece(i, s_mixc[2 + i], macc, c_recv, M_MIXH, h_send, h_recv) for i in (0, 1)]

    s_cotf = []
    for i in range(2):
        s_coth[i].wait_recv()
        s_cotf.append(send(
            M_COTF + i, cot.at[COT[i], pl.ds(HALF, HALF)],
            cot.at[pl.ds(TOK + 96 * i, (96, 160)[i]), pl.ds(HALF, HALF)], core,
        ))
    ld_cot.wait()

    def go_tiles(b):
        def body(j, _):
            go[pl.ds(b * TOK, TOK), lanes(j, 256)] = dot_t(
                cot[pl.ds(b * TOK, TOK), :], wo[lanes(j, 256), :]
            ).astype(BF16)
            return 0

        lax.fori_loop(0, 2, body, 0)

    go_tiles(0)
    s_cotc.wait_recv()
    for cp in s_cotf:
        cp.wait_recv()
    go_tiles(1)

    def backward(pair, i):
        h = 2 * pair + i
        hcol = lanes(h, 128)
        vcol = pl.ds(pl.multiple_of(h * 128 + WID, 128), 128)
        for b in range(2):
            q = qb[pl.ds(b * TOK, TOK), hcol]
            g = go[pl.ds(b * TOK, TOK), hcol]
            it = h * 2 + b
            scales = [fin[it, gr : gr + 1, :] for gr in range(5)]
            rd = None
            for gr, first, size in chunks:
                gp = dot_t(source(first, size, b, h, 1), g)
                GP[pl.ds(first, size), :] = gp
                p = E[it, pl.ds(first, size), :] * scales[gr]
                part = jnp.sum(p * gp, axis=0, keepdims=True)
                rd = part if rd is None else rd + part
            dqt = None
            for gr, first, size in chunks:
                p = E[it, pl.ds(first, size), :] * scales[gr]
                dl = (p * (GP[pl.ds(first, size), :] - rd) * SCALE).astype(BF16)
                dvv = dot(p.astype(BF16), g)
                dkk = dot(dl, q)
                part = t_dot(source(first, size, b, h, 0), dl)
                dqt = part if dqt is None else dqt + part
                if first == 0:
                    dkv[pl.ds(b * TOK, TOK), hcol] = dkk
                    dkv[pl.ds(b * TOK, TOK), vcol] = dvv
                elif first == 256:
                    dp0[pl.ds((1 - b) * 128, 128), hcol] = dkk
                    dp0[pl.ds((1 - b) * 128, 128), vcol] = dvv
                elif b == 0:
                    dS[pl.ds(first - 384, size), hcol] = dkk
                    dS[pl.ds(first - 384, size), vcol] = dvv
                else:
                    dkk = dkk + dS[pl.ds(first - 384, size), hcol]
                    dvv = dvv + dS[pl.ds(first - 384, size), vcol]
                    dS[pl.ds(first - 384, size), hcol] = dkk
                    dS[pl.ds(first - 384, size), vcol] = dvv
                    if first > 384:
                        sb[pair, pl.ds(first - 384, size), lanes(i, 128)] = dkk.astype(BF16)
                        sb[pair, pl.ds(first - 384, size), lanes(i + 2, 128)] = dvv.astype(BF16)
            dq[pl.ds(b * TOK, TOK), hcol] = dqt.T.astype(BF16)

    def heads(pair):
        def body(i, _):
            backward(pair, i)
            return 0

        lax.fori_loop(0, 2, body, 0)

    b_z = {0: [], 1: []}

    def send_z(pair, dx):
        for k in (1, 2, 3):
            for base, r in ((B_Z, level_region(k, dx)), (B_ZY, plane_region(k, dx))):
                n = base + 4 * (k - 1) + 2 * dx + pair
                b_z[dx].append(send(n, rows(sb.at[pair], r), rows(RS.at[pair], r), zdev[k]))

    heads(0)
    send_z(0, 1)
    heads(1)
    send_z(1, 1)
    send_z(0, 0)
    send_z(1, 0)

    for b in range(2):
        gk[pl.ds(b * TOK, TOK), :] = (
            spread(dp0[pl.ds(b * 128, 128), :]) + dkv[pl.ds(b * TOK, TOK), :]
        ).astype(BF16)

    def in_early(j, _):
        acc[:, lanes(j, 256)] = dot_t(dq[...], w[lanes(j, 256), pl.ds(2 * WID, WID)]) + dot_t(
            gk[...], w[lanes(j, 256), pl.ds(0, 2 * WID)]
        )
        return 0

    def returned(region):
        a, b = RS[0, pl.ds(*region), :], RS[1, pl.ds(*region), :]
        return jnp.concatenate([a[:, :256], b[:, :256], a[:, 256:], b[:, 256:]], axis=1).astype(F32)

    def collect(dx):
        for cp in b_z[dx]:
            cp.wait_recv()
        low = returned(level_region(2, dx)) + returned(level_region(3, dx))
        top = spread(low) + returned(level_region(1, dx))
        plane = dS[pl.ds(*plane_region(0, dx)), :]
        for k in (1, 2, 3):
            plane = plane + returned(plane_region(k, dx))
        return top, plane

    for i in range(4):
        s_mixc[i].wait_send()

    def in_piece(i):
        lax.fori_loop(2 * i, 2 * i + 2, in_early, 0)
        c_send[i] = acc[pl.ds(TOK, TOK), cols(i)].astype(BF16)
        return send(M_INC + i, c_send.at[i], ic_recv.at[i], core)

    def early_piece(i):
        return head_piece(i, s_inc[2 + i], acc, ic_recv, M_INH, ih_send, ih_recv)

    s_inc = {i: in_piece(i) for i in (2, 3)}
    s_inh = [early_piece(0)]

    def send_y(dx, plane):
        gy_s[dx, 0] = plane[0:16].astype(BF16)
        high = spread(plane[16:32])
        gy_s[dx, 1] = high[0:16].astype(BF16)
        gy_s[dx, 2] = high[16:32].astype(BF16)
        return [
            send(B_Y + 3 * dx + k - 1, gy_s.at[dx, k - 1], gy_r.at[dx, k - 1], ydev[k]) for k in (1, 2, 3)
        ]

    def add_y(dx, top):
        for cp in b_y[dx]:
            cp.wait_recv()
        g4 = gy_r[dx, 0].astype(F32) + gy_r[dx, 1].astype(F32) + gy_r[dx, 2].astype(F32)
        return top + spread(spread(g4))

    b_y = {}
    top, plane = collect(1)
    b_y[1] = send_y(1, plane)
    pf[pl.ds(0, 64), :] = top
    top = add_y(1, pf[pl.ds(0, 64), :])
    xa_s[...] = (spread(top) + dS[pl.ds(0, 128), :]).astype(BF16)
    b_xa = send(B_XA, xa_s, xa_r, xhi)
    s_inh.append(early_piece(1))
    s_inc.update({i: in_piece(i) for i in (0, 1)})
    top, plane = collect(0)
    b_y[0] = send_y(0, plane)
    pf[pl.ds(64, 64), :] = top

    for i in (0, 1):
        s_mixc[i].wait_recv()
        s_mixh[i].wait_recv()
        last_piece(i, macc, c_recv, h_recv)
    st_mix = load(out_b, mix_o)

    low = spread(add_y(0, pf[pl.ds(64, 64), :]))
    b_xa.wait_recv()
    low = low + xa_r[...].astype(F32)
    low = low.astype(BF16)
    out_i = lax.broadcasted_iota(jnp.int32, (TOK, 64), 0)
    inp_i = lax.broadcasted_iota(jnp.int32, (TOK, 64), 1)
    quarter = jnp.where(out_i // 4 == inp_i, 0.25, 0.0).astype(BF16)

    def late_piece(i):
        late = dot_t(low, w[cols(i), pl.ds(0, 2 * WID)])
        lacc[:, cols(i)] = late[0:64]
        lc_send[i] = late[64:128].astype(BF16)
        return send(M_LC + i, lc_send.at[i], lc_recv.at[i], core)

    def late_head(i):
        s_lc[2 + i].wait_recv()
        lh_send[i] = (lacc[:, cols(2 + i)] + lc_recv[2 + i].astype(F32)).astype(BF16)
        return send(M_LH + i, lh_send.at[i], lh_recv.at[i], head)

    s_lc = {i: late_piece(i) for i in (2, 3)}
    s_lh = [late_head(0)]
    s_lc[0] = late_piece(0)
    s_lh.append(late_head(1))
    s_lc[1] = late_piece(1)
    st_mix.wait()
    for i in (0, 1):
        s_inc[i].wait_recv()
        s_inh[i].wait_recv()
        acc[pl.ds(0, TOK), cols(i)] += ic_recv[i].astype(F32) + ih_recv[i].astype(F32)
    st_in = []
    for i in (0, 1):
        s_lc[i].wait_recv()
        s_lh[i].wait_recv()
        late = lacc[:, cols(i)] + lc_recv[i].astype(F32) + lh_recv[i].astype(F32)
        out_b[:, cols(i)] = (acc[pl.ds(0, TOK), cols(i)] + dot(quarter, late.astype(BF16))).astype(BF16)
        st_in.append(load(out_b.at[:, cols(i)], ing_o.at[:, cols(i)]))

    for i in (0, 1):
        s_mixh[i].wait_send()
    for cp in s_lh + list(s_lc.values()):
        cp.wait_send()
    for cp in s_tok + s_coth + s_cotf + s_inh + list(s_inc.values()) + [s_cotc, m_x2, b_xa]:
        cp.wait_send()
    for cp in m_x1 + m_y + m_zo + m_zw + m_zx + m_zy + b_y[0] + b_y[1] + b_z[0] + b_z[1]:
        cp.wait_send()
    for cp in st_in:
        cp.wait()


def copy_out(a, b, a_o, b_o):
    a_o[...] = a[...]
    b_o[...] = b[...]


def per_device(tokens, w_query, w_key, w_value, w_out, cotangent):
    V = pltpu.VMEM
    scratch = [
        V((2 * TOK, 2 * HALF), BF16),
        V((2 * HALF, 3 * WID), BF16),
        V((WID, 2 * HALF), BF16),
        V((2 * TOK, 2 * HALF), BF16),
        V((2 * TOK, 2 * WID), BF16),
        V((2 * TOK, WID), BF16),
        V((2 * TOK, WID), BF16),
        V((256, 2 * WID), BF16),
        V((128, 2 * WID), BF16),
        V((64, 2 * WID), BF16),
        V((32, 2 * WID), BF16),
        V((16, 2 * WID), BF16),
        V((32, 2 * WID), BF16),
        V((64, 2 * WID), BF16),
        V((32, 2 * WID), BF16),
        V((3, 16, 2 * WID), BF16),
        V((ROWS, 2 * WID), BF16),
        V((128, 2 * WID), F32),
        V((8, 1024, 256), F32),
        V((5, 8, 8, 256), F32),
        V((8, 8, 256), F32),
        V((1024, 256), F32),
        V((256, 256), F32),
        V((2 * TOK, WID), BF16),
        V((2 * TOK, 2 * HALF), F32),
        V((TOK, 2 * HALF), F32),
        V((4, TOK, 512), BF16),
        V((4, TOK, 512), BF16),
        V((2, TOK, 512), BF16),
        V((2, TOK, 512), BF16),
        V((4, TOK, 512), BF16),
        V((2, TOK, 512), BF16),
        V((2, TOK, 512), BF16),
        V((64, 2 * HALF), F32),
        V((4, 64, 512), BF16),
        V((4, 64, 512), BF16),
        V((2, 64, 512), BF16),
        V((2, 64, 512), BF16),
        V((2 * TOK, 2 * WID), F32),
        V((256, 2 * WID), F32),
        V((ROWS, 2 * WID), F32),
        V((2, ROWS, WID), BF16),
        V((2, ROWS, WID), BF16),
        V((128, 2 * WID), BF16),
        V((128, 2 * WID), BF16),
        V((2, 3, 16, 2 * WID), BF16),
        V((2, 3, 16, 2 * WID), BF16),
        V((2 * TOK, WID), BF16),
        V((2 * TOK, 2 * WID), BF16),
        V((TOK, HALF), BF16),
        pltpu.SemaphoreType.DMA((16,)),
        pltpu.SemaphoreType.DMA((N_MSG,)),
        pltpu.SemaphoreType.DMA((N_MSG,)),
    ]
    any_spec = pl.BlockSpec(memory_space=pl.ANY)
    out = jax.ShapeDtypeStruct((TOK, HALF), BF16)
    mixed, input_grad = pl.pallas_call(
        kernel,
        out_shape=(out, out),
        in_specs=[any_spec] * 6,
        out_specs=(any_spec, any_spec),
        scratch_shapes=scratch,
        compiler_params=pltpu.CompilerParams(
            collective_id=0, has_side_effects=True, vmem_limit_bytes=60 * 2**20
        ),
    )(tokens, w_query, w_key, w_value, w_out, cotangent)
    return pl.pallas_call(
        copy_out,
        grid=(2,),
        out_shape=(out, out),
        in_specs=[pl.BlockSpec((TOK // 2, HALF), lambda i: (i, 0))] * 2,
        out_specs=[pl.BlockSpec((TOK // 2, HALF), lambda i: (i, 0))] * 2,
    )(mixed, input_grad)


def solution(mesh):
    return jax.shard_map(
        per_device,
        mesh=mesh,
        in_specs=(
            P("seq", None), P(None, "head"), P(None, "head"), P(None, "head"),
            P("head", None), P("seq", "head"),
        ),
        out_specs=(P("seq", "head"), P("seq", "head")),
        check_vma=False,
    )
```

```python
import functools
import math

import jax
import jax.numpy as jnp
from jax import lax
from jax.experimental import pallas as pl
from jax.experimental.pallas import tpu as pltpu
from jax.sharding import PartitionSpec as P

MESH = pl.DeviceIdType.MESH
F32 = jnp.float32
BF16 = jnp.bfloat16
LN2 = math.log(2.0)
SCALE = 1.0 / math.sqrt(128)

TOK = 256
WID = 512
HALF = 1024
ROWS = 640


def level_region(dz, dx):
    return (128 + dx * 256, 64) if dz == 1 else (128 + dx * 256 + 32 * dz, 32)


def half(region, b):
    return (region[0] + b * region[1] // 2, region[1] // 2)


def plane_region(dz, dx):
    return (256 + dx * 256 + 32 * dz, 32)


def dot(a, b):
    return jnp.dot(a, b, preferred_element_type=F32)


def dot_t(a, b):
    return lax.dot_general(a, b, (((1,), (1,)), ((), ())), preferred_element_type=F32)


def pool(value):
    n = value.shape[0]
    out = lax.broadcasted_iota(jnp.int32, (n // 2, n), 0)
    inp = lax.broadcasted_iota(jnp.int32, (n // 2, n), 1)
    return dot(jnp.where(inp // 2 == out, 0.5, 0.0).astype(BF16), value).astype(BF16)


def spread(value):
    n = value.shape[0]
    out = lax.broadcasted_iota(jnp.int32, (2 * n, n), 0)
    inp = lax.broadcasted_iota(jnp.int32, (2 * n, n), 1)
    return dot(jnp.where(out // 2 == inp, 0.5, 0.0).astype(BF16), value.astype(BF16))


def t_dot(a, b):
    return lax.dot_general(a, b, (((0,), (0,)), ((), ())), preferred_element_type=F32)


def lanes(i, width):
    return pl.ds(pl.multiple_of(i * width, width), width)


(
    M_TOK, M_COTC, M_COTH, M_COTF, M_MIXC, M_MIXH, M_INC, M_INH,
    M_Y, M_X1, M_X2, M_ZO, M_ZW, M_ZX, M_ZY,
    B_XA, B_Z, B_ZY, B_Y, M_LC, M_LH, N_MSG,
) = (0, 2, 3, 5, 7, 11, 13, 17, 19, 22, 24, 25, 31, 34, 40, 43, 44, 56, 68, 74, 78, 80)


def kernel(
    tok_h, wq_h, wk_h, wv_h, wo_h, cot_h, mix_o, ing_o,
    tok, w, wo, cot, kv, qb, go, p0, p1, p2, p3, p4, wpl, p2x, p3x, ybuf, S,
    pf, E, stat, fin, GP, ypb, att, acc, macc, c_send, c_recv, h_send, h_recv, ic_recv, ih_send, ih_recv,
    lacc, lc_send, lc_recv, lh_send, lh_recv,
    dkv, dp0, dS, sb, RS, xa_s, xa_r, gy_s, gy_r, dq, gk, out_b,
    lsem, ssem, rsem,
):
    s = lax.axis_index("seq")
    hd = lax.axis_index("head")
    c = s % 2

    def flip(bit):
        return (1 - 2 * ((s // bit) % 2)) * bit

    core = (s + flip(1), hd)
    head = (s, 1 - hd)
    xhi = (s + flip(2), hd)
    zdev = {1: (s + flip(4), hd), 2: (s + flip(8), hd), 3: (s + flip(4) + flip(8), hd)}
    ydev = {1: (s + flip(16), hd), 2: (s + flip(32), hd), 3: (s + flip(16) + flip(32), hd)}

    own = pl.ds(pl.multiple_of(hd * HALF, HALF), HALF)
    oth = pl.ds(pl.multiple_of((1 - hd) * HALF, HALF), HALF)
    wcol = pl.ds(pl.multiple_of(c * WID, WID), WID)
    halves = ((own, pl.ds(0, HALF)), (oth, pl.ds(HALF, HALF)))
    lcount = [0]

    def load(src, dst):
        cp = pltpu.make_async_copy(src, dst, lsem.at[lcount[0]])
        lcount[0] += 1
        cp.start()
        return cp

    ld_tok = [load(tok_h.at[:, a], tok.at[pl.ds(0, TOK), b]) for a, b in halves]
    ld_k = [load(wk_h.at[a, wcol], w.at[b, pl.ds(0, WID)]) for a, b in halves]
    ld_v = [load(wv_h.at[a, wcol], w.at[b, pl.ds(WID, WID)]) for a, b in halves]

    barrier = pltpu.get_barrier_semaphore()
    partners = [core, head, xhi] + [zdev[k] for k in (1, 2, 3)] + [ydev[k] for k in (1, 2, 3)]
    for d in partners:
        pl.semaphore_signal(barrier, inc=1, device_id=d, device_id_type=MESH)
    pl.semaphore_wait(barrier, len(partners))

    def send(n, src, dst, dev):
        cp = pltpu.make_async_remote_copy(
            src_ref=src, dst_ref=dst, send_sem=ssem.at[n], recv_sem=rsem.at[n],
            device_id=dev, device_id_type=MESH,
        )
        cp.start()
        return cp

    def rows(ref, region):
        return ref.at[pl.ds(*region)]

    s_tok = [
        send(M_TOK + i, tok_h.at[:, a], tok.at[pl.ds(TOK, TOK), b], core)
        for i, (a, b) in enumerate(halves)
    ]
    COT = [pl.ds(0, 96), pl.ds(96, 160)]

    def send_cot(i):
        part = COT[i]
        return send(M_COTH + i, cot_h.at[part], cot.at[part, pl.ds(HALF, HALF)], head)

    s_coth = [send_cot(0)]

    for cp in ld_tok + ld_k + ld_v:
        cp.wait()
    ld_q = [load(wq_h.at[a, wcol], w.at[b, pl.ds(2 * WID, WID)]) for a, b in halves]
    ld_cot = load(cot_h, cot.at[pl.ds(0, TOK), pl.ds(0, HALF)])
    ld_o = [load(wo_h.at[wcol, a], wo.at[:, b]) for a, b in halves]

    def kv_tiles(b):
        def body(j, _):
            r = dot(tok[pl.ds(b * TOK, TOK), :], w[:, lanes(j, 512)]).astype(BF16)
            kv[pl.ds(b * TOK, TOK), lanes(j, 512)] = r
            return 0

        lax.fori_loop(0, 2, body, 0)

    m_x1, m_zo, m_zx = [], [], []

    def pool_block(b):
        p0[pl.ds(b * 128, 128), :] = pool(kv[pl.ds(b * TOK, TOK), :])
        p1[pl.ds(b * 64, 64), :] = pool(p0[pl.ds(b * 128, 128), :])
        m_x1.append(send(M_X1 + b, rows(p1, (b * 64, 64)), rows(S, (b * 64, 64)), xhi))
        p2[pl.ds(b * 32, 32), :] = pool(p1[pl.ds(b * 64, 64), :])
        p3[pl.ds(b * 16, 16), :] = pool(p2[pl.ds(b * 32, 32), :])
        m_zo.extend(pass_z(M_ZO, b, 0, p2, p3))

    def pass_z(base, b, dx, two, three):
        out = []
        for k in (1, 2, 3):
            src = rows(two, (b * 32, 32)) if k == 1 else rows(three, (b * 16, 16))
            out.append(send(base + 2 * (k - 1) + b, src, rows(S, half(level_region(k, dx), b)), zdev[k]))
        return out

    kv_tiles(0)
    pool_block(0)
    for cp in s_tok:
        cp.wait_recv()
    s_cotc = send(M_COTC, cot_h, cot.at[pl.ds(TOK, TOK), pl.ds(0, HALF)], core)
    kv_tiles(1)
    pool_block(1)
    p4[...] = pool(p3[...])
    m_y = [send(M_Y + k - 1, p4, ybuf.at[k - 1], ydev[k]) for k in (1, 2, 3)]

    for cp in ld_q:
        cp.wait()

    def q_body(j, _):
        qb[:, lanes(j, 256)] = dot(tok[...], w[:, pl.ds(pl.multiple_of(2 * WID + j * 256, 256), 256)]).astype(BF16)
        return 0

    lax.fori_loop(0, 2, q_body, 0)

    groups = [
        [(0, 256, 0.0), (256, 128, LN2)],
        [(384, 128, 2 * LN2)],
        [(512, 256, None)],
        [(768, 128, None)],
        [(896, 128, None)],
    ]
    chunks = [(gr, first, size) for gr in range(5) for first, size, _ in groups[gr]]
    r_iota = lax.broadcasted_iota(jnp.int32, (256, 256), 0)
    r_level = jnp.where(r_iota < 64, 3, jnp.where(r_iota < 128, 4, 5 + (r_iota // 16) % 2))
    ypb[...] = r_level.astype(F32) * LN2

    def source(first, size, b, h, value):
        col = pl.ds(pl.multiple_of(h * 128 + value * WID, 128), 128)
        if first == 0:
            return kv[pl.ds(b * TOK, TOK), col]
        if first == 256:
            return p0[pl.ds((1 - b) * 128, 128), col]
        return S[pl.ds(first - 384, size), col]

    def score(gr, h, b):
        it = h * 2 + b
        q = qb[pl.ds(b * TOK, TOK), lanes(h, 128)]
        parts = []
        peak = None
        for first, size, bias in groups[gr]:
            l = dot_t(source(first, size, b, h, 0), q) * SCALE
            if bias is None:
                l = l + ypb[pl.ds((first - 512) % 256, size), :]
            elif bias:
                l = l + bias
            parts.append(l)
            top = jnp.max(l, axis=0, keepdims=True)
            peak = top if peak is None else jnp.maximum(peak, top)
        total = None
        for (first, size, _), l in zip(groups[gr], parts):
            e = jnp.exp(l - peak)
            E[it, pl.ds(first, size), :] = e
            part = jnp.sum(e, axis=0, keepdims=True)
            total = part if total is None else total + part
        stat[gr, it, 0:1, :] = peak
        stat[gr, it, 1:2, :] = total

    def each(*steps):
        def body(h, _):
            for b in range(2):
                for f, gr in steps:
                    f(gr, h, b)
            return 0

        lax.fori_loop(0, 4, body, 0)

    for cp in m_y:
        cp.wait_recv()
    wpl[pl.ds(0, 16), :] = ybuf[0]
    wpl[pl.ds(16, 16), :] = pool(jnp.concatenate([ybuf[1], ybuf[2]], axis=0))
    m_x2 = send(M_X2, wpl, rows(S, plane_region(0, 1)), xhi)
    m_zw = [send(M_ZW + k - 1, wpl, rows(S, plane_region(k, 0)), zdev[k]) for k in (1, 2, 3)]
    S[pl.ds(*plane_region(0, 0)), :] = wpl[...]

    def pass_x(b):
        m_x1[b].wait_recv()
        p2x[pl.ds(b * 32, 32), :] = pool(S[pl.ds(b * 64, 64), :])
        p3x[pl.ds(b * 16, 16), :] = pool(p2x[pl.ds(b * 32, 32), :])
        m_zx.extend(pass_z(M_ZX, b, 1, p2x, p3x))

    pass_x(0)
    each((score, 0))
    pass_x(1)
    m_x2.wait_recv()
    s_coth.append(send_cot(1))
    m_zy = [
        send(M_ZY + k - 1, rows(S, plane_region(0, 1)), rows(S, plane_region(k, 1)), zdev[k])
        for k in (1, 2, 3)
    ]

    for cp in m_zo + m_zw:
        cp.wait_recv()
    each((score, 1), (score, 2))

    for cp in m_zx:
        cp.wait_recv()
    each((score, 3))
    for cp in m_zy:
        cp.wait_recv()

    for cp in ld_o:
        cp.wait()

    def finish(h, _):
        for b in range(2):
            it = h * 2 + b
            score(4, h, b)
            peaks = [stat[gr, it, 0:1, :] for gr in range(5)]
            peak = functools.reduce(jnp.maximum, peaks)
            scales = [jnp.exp(m - peak) for m in peaks]
            total = sum(f * stat[gr, it, 1:2, :] for gr, f in enumerate(scales))
            scales = [f / total for f in scales]
            for gr, f in enumerate(scales):
                fin[it, gr : gr + 1, :] = f
            a = None
            for gr, first, size in chunks:
                pb = (E[it, pl.ds(first, size), :] * scales[gr]).astype(BF16)
                part = t_dot(source(first, size, b, h, 1), pb)
                a = part if a is None else a + part
            att[pl.ds(b * TOK, TOK), lanes(h, 128)] = a.T.astype(BF16)
        return 0

    lax.fori_loop(0, 4, finish, 0)

    def cols(i):
        return pl.ds(i * 512, 512)

    def out_piece(i):
        c_send[i] = dot(att[pl.ds(TOK, TOK), :], wo[:, cols(i)]).astype(BF16)
        cp = send(M_MIXC + i, c_send.at[i], c_recv.at[i], core)
        macc[:, cols(i)] = dot(att[pl.ds(0, TOK), :], wo[:, cols(i)])
        return cp

    def head_piece(i, cp, total, got, base, src, dst):
        cp.wait_recv()
        src[i] = (total[pl.ds(0, TOK), cols(2 + i)] + got[2 + i].astype(F32)).astype(BF16)
        return send(base + i, src.at[i], dst.at[i], head)

    def last_piece(i, total, got, got_h):
        out_b[:, cols(i)] = (
            total[pl.ds(0, TOK), cols(i)] + got[i].astype(F32) + got_h[i].astype(F32)
        ).astype(BF16)

    s_mixc = {i: out_piece(i) for i in (2, 3, 0, 1)}
    s_mixh = [head_piece(i, s_mixc[2 + i], macc, c_recv, M_MIXH, h_send, h_recv) for i in (0, 1)]

    s_cotf = []
    for i in range(2):
        s_coth[i].wait_recv()
        s_cotf.append(send(
            M_COTF + i, cot.at[COT[i], pl.ds(HALF, HALF)],
            cot.at[pl.ds(TOK + 96 * i, (96, 160)[i]), pl.ds(HALF, HALF)], core,
        ))
    ld_cot.wait()

    def go_tiles(b):
        def body(j, _):
            go[pl.ds(b * TOK, TOK), lanes(j, 256)] = dot_t(
                cot[pl.ds(b * TOK, TOK), :], wo[lanes(j, 256), :]
            ).astype(BF16)
            return 0

        lax.fori_loop(0, 2, body, 0)

    go_tiles(0)
    s_cotc.wait_recv()
    for cp in s_cotf:
        cp.wait_recv()
    go_tiles(1)

    def backward(pair, i):
        h = 2 * pair + i
        hcol = lanes(h, 128)
        vcol = pl.ds(pl.multiple_of(h * 128 + WID, 128), 128)
        for b in range(2):
            q = qb[pl.ds(b * TOK, TOK), hcol]
            g = go[pl.ds(b * TOK, TOK), hcol]
            it = h * 2 + b
            scales = [fin[it, gr : gr + 1, :] for gr in range(5)]
            rd = None
            for gr, first, size in chunks:
                gp = dot_t(source(first, size, b, h, 1), g)
                GP[pl.ds(first, size), :] = gp
                p = E[it, pl.ds(first, size), :] * scales[gr]
                part = jnp.sum(p * gp, axis=0, keepdims=True)
                rd = part if rd is None else rd + part
            dqt = None
            for gr, first, size in chunks:
                p = E[it, pl.ds(first, size), :] * scales[gr]
                dl = (p * (GP[pl.ds(first, size), :] - rd) * SCALE).astype(BF16)
                dvv = dot(p.astype(BF16), g)
                dkk = dot(dl, q)
                part = t_dot(source(first, size, b, h, 0), dl)
                dqt = part if dqt is None else dqt + part
                if first == 0:
                    dkv[pl.ds(b * TOK, TOK), hcol] = dkk
                    dkv[pl.ds(b * TOK, TOK), vcol] = dvv
                elif first == 256:
                    dp0[pl.ds((1 - b) * 128, 128), hcol] = dkk
                    dp0[pl.ds((1 - b) * 128, 128), vcol] = dvv
                elif b == 0:
                    dS[pl.ds(first - 384, size), hcol] = dkk
                    dS[pl.ds(first - 384, size), vcol] = dvv
                else:
                    dkk = dkk + dS[pl.ds(first - 384, size), hcol]
                    dvv = dvv + dS[pl.ds(first - 384, size), vcol]
                    dS[pl.ds(first - 384, size), hcol] = dkk
                    dS[pl.ds(first - 384, size), vcol] = dvv
                    if first > 384:
                        sb[pair, pl.ds(first - 384, size), lanes(i, 128)] = dkk.astype(BF16)
                        sb[pair, pl.ds(first - 384, size), lanes(i + 2, 128)] = dvv.astype(BF16)
            dq[pl.ds(b * TOK, TOK), hcol] = dqt.T.astype(BF16)

    def heads(pair):
        def body(i, _):
            backward(pair, i)
            return 0

        lax.fori_loop(0, 2, body, 0)

    b_z = {0: [], 1: []}

    def send_z(pair, dx):
        for k in (1, 2, 3):
            for base, r in ((B_Z, level_region(k, dx)), (B_ZY, plane_region(k, dx))):
                n = base + 4 * (k - 1) + 2 * dx + pair
                b_z[dx].append(send(n, rows(sb.at[pair], r), rows(RS.at[pair], r), zdev[k]))

    heads(0)
    send_z(0, 1)
    heads(1)
    send_z(1, 1)
    send_z(0, 0)
    send_z(1, 0)

    for b in range(2):
        gk[pl.ds(b * TOK, TOK), :] = (
            spread(dp0[pl.ds(b * 128, 128), :]) + dkv[pl.ds(b * TOK, TOK), :]
        ).astype(BF16)

    def in_early(j, _):
        acc[:, lanes(j, 256)] = dot_t(dq[...], w[lanes(j, 256), pl.ds(2 * WID, WID)]) + dot_t(
            gk[...], w[lanes(j, 256), pl.ds(0, 2 * WID)]
        )
        return 0

    def returned(region):
        a, b = RS[0, pl.ds(*region), :], RS[1, pl.ds(*region), :]
        return jnp.concatenate([a[:, :256], b[:, :256], a[:, 256:], b[:, 256:]], axis=1).astype(F32)

    def collect(dx):
        for cp in b_z[dx]:
            cp.wait_recv()
        low = returned(level_region(2, dx)) + returned(level_region(3, dx))
        top = spread(low) + returned(level_region(1, dx))
        plane = dS[pl.ds(*plane_region(0, dx)), :]
        for k in (1, 2, 3):
            plane = plane + returned(plane_region(k, dx))
        return top, plane

    for i in range(4):
        s_mixc[i].wait_send()

    def in_piece(i):
        lax.fori_loop(2 * i, 2 * i + 2, in_early, 0)
        c_send[i] = acc[pl.ds(TOK, TOK), cols(i)].astype(BF16)
        return send(M_INC + i, c_send.at[i], ic_recv.at[i], core)

    def early_piece(i):
        return head_piece(i, s_inc[2 + i], acc, ic_recv, M_INH, ih_send, ih_recv)

    s_inc = {i: in_piece(i) for i in (2, 3)}
    s_inh = [early_piece(0)]

    def send_y(dx, plane):
        gy_s[dx, 0] = plane[0:16].astype(BF16)
        high = spread(plane[16:32])
        gy_s[dx, 1] = high[0:16].astype(BF16)
        gy_s[dx, 2] = high[16:32].astype(BF16)
        return [
            send(B_Y + 3 * dx + k - 1, gy_s.at[dx, k - 1], gy_r.at[dx, k - 1], ydev[k]) for k in (1, 2, 3)
        ]

    def add_y(dx, top):
        for cp in b_y[dx]:
            cp.wait_recv()
        g4 = gy_r[dx, 0].astype(F32) + gy_r[dx, 1].astype(F32) + gy_r[dx, 2].astype(F32)
        return top + spread(spread(g4))

    b_y = {}
    top, plane = collect(1)
    b_y[1] = send_y(1, plane)
    pf[pl.ds(0, 64), :] = top
    top = add_y(1, pf[pl.ds(0, 64), :])
    xa_s[...] = (spread(top) + dS[pl.ds(0, 128), :]).astype(BF16)
    b_xa = send(B_XA, xa_s, xa_r, xhi)
    s_inh.append(early_piece(1))
    s_inc.update({i: in_piece(i) for i in (0, 1)})
    top, plane = collect(0)
    b_y[0] = send_y(0, plane)
    pf[pl.ds(64, 64), :] = top

    for i in (0, 1):
        s_mixc[i].wait_recv()
        s_mixh[i].wait_recv()
        last_piece(i, macc, c_recv, h_recv)
    st_mix = load(out_b, mix_o)

    low = spread(add_y(0, pf[pl.ds(64, 64), :]))
    b_xa.wait_recv()
    low = low + xa_r[...].astype(F32)
    low = low.astype(BF16)
    out_i = lax.broadcasted_iota(jnp.int32, (TOK, 64), 0)
    inp_i = lax.broadcasted_iota(jnp.int32, (TOK, 64), 1)
    quarter = jnp.where(out_i // 4 == inp_i, 0.25, 0.0).astype(BF16)

    def late_piece(i):
        late = dot_t(low, w[cols(i), pl.ds(0, 2 * WID)])
        lacc[:, cols(i)] = late[0:64]
        lc_send[i] = late[64:128].astype(BF16)
        return send(M_LC + i, lc_send.at[i], lc_recv.at[i], core)

    def late_head(i):
        s_lc[2 + i].wait_recv()
        lh_send[i] = (lacc[:, cols(2 + i)] + lc_recv[2 + i].astype(F32)).astype(BF16)
        return send(M_LH + i, lh_send.at[i], lh_recv.at[i], head)

    s_lc = {i: late_piece(i) for i in (2, 3)}
    s_lh = [late_head(0)]
    s_lc[0] = late_piece(0)
    s_lh.append(late_head(1))
    s_lc[1] = late_piece(1)
    st_mix.wait()
    for i in (0, 1):
        s_inc[i].wait_recv()
        s_inh[i].wait_recv()
        acc[pl.ds(0, TOK), cols(i)] += ic_recv[i].astype(F32) + ih_recv[i].astype(F32)
    st_in = []
    for i in (0, 1):
        s_lc[i].wait_recv()
        s_lh[i].wait_recv()
        late = lacc[:, cols(i)] + lc_recv[i].astype(F32) + lh_recv[i].astype(F32)
        out_b[:, cols(i)] = (acc[pl.ds(0, TOK), cols(i)] + dot(quarter, late.astype(BF16))).astype(BF16)
        st_in.append(load(out_b.at[:, cols(i)], ing_o.at[:, cols(i)]))

    for i in (0, 1):
        s_mixh[i].wait_send()
    for cp in s_lh + list(s_lc.values()):
        cp.wait_send()
    for cp in s_tok + s_coth + s_cotf + s_inh + list(s_inc.values()) + [s_cotc, m_x2, b_xa]:
        cp.wait_send()
    for cp in m_x1 + m_y + m_zo + m_zw + m_zx + m_zy + b_y[0] + b_y[1] + b_z[0] + b_z[1]:
        cp.wait_send()
    for cp in st_in:
        cp.wait()


def copy_out(a, b, a_o, b_o):
    a_o[...] = a[...]
    b_o[...] = b[...]


def per_device(tokens, w_query, w_key, w_value, w_out, cotangent):
    V = pltpu.VMEM
    scratch = [
        V((2 * TOK, 2 * HALF), BF16),
        V((2 * HALF, 3 * WID), BF16),
        V((WID, 2 * HALF), BF16),
        V((2 * TOK, 2 * HALF), BF16),
        V((2 * TOK, 2 * WID), BF16),
        V((2 * TOK, WID), BF16),
        V((2 * TOK, WID), BF16),
        V((256, 2 * WID), BF16),
        V((128, 2 * WID), BF16),
        V((64, 2 * WID), BF16),
        V((32, 2 * WID), BF16),
        V((16, 2 * WID), BF16),
        V((32, 2 * WID), BF16),
        V((64, 2 * WID), BF16),
        V((32, 2 * WID), BF16),
        V((3, 16, 2 * WID), BF16),
        V((ROWS, 2 * WID), BF16),
        V((128, 2 * WID), F32),
        V((8, 1024, 256), F32),
        V((5, 8, 8, 256), F32),
        V((8, 8, 256), F32),
        V((1024, 256), F32),
        V((256, 256), F32),
        V((2 * TOK, WID), BF16),
        V((2 * TOK, 2 * HALF), F32),
        V((TOK, 2 * HALF), F32),
        V((4, TOK, 512), BF16),
        V((4, TOK, 512), BF16),
        V((2, TOK, 512), BF16),
        V((2, TOK, 512), BF16),
        V((4, TOK, 512), BF16),
        V((2, TOK, 512), BF16),
        V((2, TOK, 512), BF16),
        V((64, 2 * HALF), F32),
        V((4, 64, 512), BF16),
        V((4, 64, 512), BF16),
        V((2, 64, 512), BF16),
        V((2, 64, 512), BF16),
        V((2 * TOK, 2 * WID), F32),
        V((256, 2 * WID), F32),
        V((ROWS, 2 * WID), F32),
        V((2, ROWS, WID), BF16),
        V((2, ROWS, WID), BF16),
        V((128, 2 * WID), BF16),
        V((128, 2 * WID), BF16),
        V((2, 3, 16, 2 * WID), BF16),
        V((2, 3, 16, 2 * WID), BF16),
        V((2 * TOK, WID), BF16),
        V((2 * TOK, 2 * WID), BF16),
        V((TOK, HALF), BF16),
        pltpu.SemaphoreType.DMA((16,)),
        pltpu.SemaphoreType.DMA((N_MSG,)),
        pltpu.SemaphoreType.DMA((N_MSG,)),
    ]
    any_spec = pl.BlockSpec(memory_space=pl.ANY)
    out = jax.ShapeDtypeStruct((TOK, HALF), BF16)
    mixed, input_grad = pl.pallas_call(
        kernel,
        out_shape=(out, out),
        in_specs=[any_spec] * 6,
        out_specs=(any_spec, any_spec),
        scratch_shapes=scratch,
        compiler_params=pltpu.CompilerParams(
            collective_id=0, has_side_effects=True, vmem_limit_bytes=60 * 2**20
        ),
    )(tokens, w_query, w_key, w_value, w_out, cotangent)
    return pl.pallas_call(
        copy_out,
        grid=(2,),
        out_shape=(out, out),
        in_specs=[pl.BlockSpec((TOK // 2, HALF), lambda i: (i, 0))] * 2,
        out_specs=[pl.BlockSpec((TOK // 2, HALF), lambda i: (i, 0))] * 2,
    )(mixed, input_grad)


def solution(mesh):
    return jax.shard_map(
        per_device,
        mesh=mesh,
        in_specs=(
            P("seq", None), P(None, "head"), P(None, "head"), P(None, "head"),
            P("head", None), P("seq", "head"),
        ),
        out_specs=(P("seq", "head"), P("seq", "head")),
        check_vma=False,
    )
```
